512 devices in a mesh: row: 32 (over z, core), col: 16 (over y, x).
Axes of the slice: x: 4, y: 4, z: 16, core: 2. Of those that a mesh axis runs over, the one named last changes fastest.
Arguments:
- tokens: bfloat16 [384, 14336], P('row', 'col'), may hold values from -6 to 6
- w_in: bfloat16 [14336, 40960], P('col', 'row'), may hold values from -0.046875 to 0.046875
- b_in: float32 [40960], P('row'), may hold values from -3 to 3
- w_out: bfloat16 [40960, 14336], P('row', 'col'), may hold values from -0.03125 to 0.03125
- b_out: float32 [14336], P('col'), may hold values from -3 to 3
Outputs:
- block_out: bfloat16 [384, 14336], P('row', 'col')
The draws below stay inside these ranges and needn't reach their ends.
All inputs are finite; a program needn't handle non-finite values.
Results may differ from the reference program's by a relative error of at most 0.0044.
Values may be sent and summed in bfloat16 or wider, within the bound.
A program may use at most 64 MiB of HBM per device.

```python
import jax
import jax.numpy as jnp

D = 14336
FW = 40960
TOKENS = 384


def block_levels(stream_key, dims, cuts, smallest, largest):
    def one(dim, parts):
        heights = jax.random.uniform(jax.random.fold_in(jax.random.fold_in(stream_key, 6), dim), (parts,), jnp.float32, smallest / len(cuts), largest / len(cuts))
        return jnp.repeat(jnp.exp(heights), dims[dim] // parts).reshape((-1,) + (1,) * (len(dims) - dim - 1))

    loudness = one(*cuts[0])
    for cut in cuts[1:]:
        loudness = loudness * one(*cut)
    return loudness


def normal_values(rng, extent, width, bound, cuts=(), kind=jnp.bfloat16):
    drawn = jax.random.normal(rng, extent, jnp.float32) * width
    if len(cuts) > 0:
        drawn = block_levels(rng, extent, cuts, -0.22, 0.18) * drawn
    return jnp.clip(drawn, min=-bound, max=bound).astype(kind)


def setup_inputs(seed: int = 0) -> dict:
    keys = jax.random.split(jax.random.key(seed), 6)
    return {
        "tokens": normal_values(keys[0], (TOKENS, D), 1.0, 6.0, ((0, 32), (1, 16))),
        "w_in": normal_values(keys[1], (D, FW), D ** -0.5, 0.046875, ((0, 16), (1, 32))),
        "b_in": normal_values(keys[2], (FW,), 0.5, 3.0, ((0, 32),), jnp.float32),
        "w_out": normal_values(keys[3], (FW, D), FW ** -0.5, 0.03125, ((0, 32), (1, 16))),
        "b_out": normal_values(keys[4], (D,), 0.5, 3.0, ((0, 16),), jnp.float32),
    }


def reference(tokens, w_in, b_in, w_out, b_out):
    pre = jnp.dot(tokens, w_in, preferred_element_type=jnp.float32) + b_in
    hidden = jax.nn.gelu(pre, approximate=True).astype(jnp.bfloat16)
    result = jnp.dot(hidden, w_out, preferred_element_type=jnp.float32)
    return (result + b_out).astype(jnp.bfloat16)
```

```python
import functools

import jax
import jax.numpy as jnp
from jax import lax
from jax.experimental import pallas as pl
from jax.experimental.pallas import tpu as pltpu
from jax.sharding import PartitionSpec as P

BF16 = jnp.bfloat16
F32 = jnp.float32
PARENT = {1: 0, 2: 0, 4: 0, 3: 2, 5: 4, 6: 4, 8: 4, 7: 6}
BASE = {1: 1, 2: 3, 4: 5, 3: 7, 5: 9, 6: 11, 7: 13, 8: 15}
PLANE = [(dy, dx) for dy in (2, 1, 3, 0) for dx in (2, 1, 3, 0) if (dy, dx) != (0, 0)]
GROUPS = 3
A_CUTS = (0, 6, 12, 16)
D_CUTS = (0, 5, 10, 16)


def slot(side, m):
    return BASE[m] + side


def kernel(
    tok_ref, win_ref, bin_ref, wout_ref, bout_ref, o_ref,
    win, wout, ta, xs, pf, pb, rb, hid, po, ss, sr, zs, zr,
    wsem, a_send, a_recv, as_send, as_recv, b_send, b_recv, c_send, c_recv,
    ds_send, ds_recv, d_send, d_recv,
):
    row, col = lax.axis_index("row"), lax.axis_index("col")
    z, c = row // 2, row % 2
    y, x = col // 4, col % 4
    half = pb.shape[-1]
    s8 = 1 - 2 * c

    def z_peer(dz):
        return {"row": lax.rem(z + dz + 16, 16) * 2 + c, "col": col}

    def plane_col(dy, dx):
        return lax.rem(y + dy + 4, 4) * 4 + lax.rem(x + dx + 4, 4)

    def plane_peer(dy, dx):
        return {"row": row, "col": plane_col(dy, dx)}

    sibling = {"row": z * 2 + (1 - c), "col": col}

    def remote(src, dst, send, recv, peer):
        return pltpu.make_async_remote_copy(
            src_ref=src, dst_ref=dst, send_sem=send, recv_sem=recv,
            device_id=peer, device_id_type=pl.DeviceIdType.MESH,
        )

    sent = []

    def start(copy):
        copy.start()
        sent.append(copy)

    load_in = pltpu.make_async_copy(win_ref, win, wsem.at[0])
    load_out = pltpu.make_async_copy(wout_ref, wout, wsem.at[1])
    load_in.start()
    load_out.start()

    barrier = pltpu.get_barrier_semaphore()
    peers = [z_peer(dz) for dz in (4, -4, 2, -2, 1, -1)]
    peers += [plane_peer(dy, dx) for dy, dx in PLANE] + [sibling]
    for peer in peers:
        pl.semaphore_signal(barrier, inc=1, device_id=peer, device_id_type=pl.DeviceIdType.MESH)

    own = tok_ref[...].astype(F32)
    tail, none = own[8:12], jnp.zeros((4, own.shape[1]), F32)
    tail = jnp.where(
        c == 0, jnp.concatenate([tail, none], axis=0), jnp.concatenate([none, tail], axis=0)
    )
    ta[c, 0] = jnp.concatenate([own[0:8], tail], axis=0).astype(BF16)
    pl.semaphore_wait(barrier, len(peers))

    def a_copy(side, m, at):
        sign = 1 - 2 * side
        dz = -sign * (m - PARENT[m])
        place = slot(side, m)
        return remote(ta.at[c, at], ta.at[c, place], a_send.at[side, m], a_recv.at[side, m], z_peer(dz))

    def a_copy8():
        return remote(ta.at[c, slot(0, 4) + c], ta.at[c, 15], a_send.at[0, 8], a_recv.at[0, 8], z_peer(-4 * s8))

    def a_wait(side, m):
        a_copy(side, m, 0).wait_recv()

    def a_sibling(g):
        part = pl.ds(A_CUTS[g], A_CUTS[g + 1] - A_CUTS[g])
        return remote(ta.at[c, part], ta.at[c, part], as_send.at[g], as_recv.at[g], sibling)

    def a_sibling_wait(g):
        part = pl.ds(A_CUTS[g], A_CUTS[g + 1] - A_CUTS[g])
        remote(ta.at[1 - c, part], ta.at[1 - c, part], as_send.at[g], as_recv.at[g], sibling).wait_recv()

    def assemble(g):
        for k in range(A_CUTS[g], A_CUTS[g + 1], 2):
            rows = []
            for i in (k, k + 1):
                first, second = ta[0, i].astype(F32), ta[1, i].astype(F32)
                rows += [first[0:8], second[0:8], first[8:16] + second[8:16]]
            xs[24 * k : 24 * k + 48, :] = jnp.concatenate(rows, axis=0).astype(BF16)

    def project_in(g):
        lhs = xs[128 * g : 128 * g + 128, :]

        @pl.loop(0, 2)
        def _(h):
            cols = pl.ds(pl.multiple_of(h * half, 128), half)
            part = jnp.dot(lhs, win[:, cols], preferred_element_type=F32).reshape(8, 16, half)
            pf[g, :, h] = part
            pb[g, :, h] = part.astype(BF16)

    def b_copy(g, dy, dx):
        there = plane_col(dy, dx)
        d = dy * 4 + dx
        return remote(
            pb.at[g, there // 2, there % 2], rb.at[g, d], b_send.at[g, d], b_recv.at[g, d], plane_peer(dy, dx)
        )

    def b_start(g):
        for dy, dx in PLANE:
            start(b_copy(g, dy, dx))

    def b_finish(g):
        total = pf[g, col // 2, col % 2]
        for dy, dx in reversed(PLANE):
            b_copy(g, dy, dx).wait_recv()
            total += rb[g, dy * 4 + dx].astype(F32)
        v = total + bin_ref[:, pl.ds(pl.multiple_of((col % 2) * half, 128), half)]
        v = 0.5 * v * (1.0 + jnp.tanh(0.7978845608 * (v + 0.044715 * (v * v * v))))
        hid[g, col // 2, col % 2] = v.astype(BF16)

    def c_start(g):
        block = hid.at[g, col // 2, col % 2]
        for dy, dx in PLANE:
            d = dy * 4 + dx
            start(remote(block, block, c_send.at[g, d], c_recv.at[g, d], plane_peer(dy, dx)))

    def c_wait(g):
        for dy, dx in reversed(PLANE):
            d = dy * 4 + dx
            there = plane_col(-dy, -dx)
            block = hid.at[g, there // 2, there % 2]
            remote(block, block, c_send.at[g, d], c_recv.at[g, d], plane_peer(-dy, -dx)).wait_recv()

    def project_out(g):
        total = jnp.zeros((128, po.shape[1]), F32)
        for h in range(2):
            lhs = hid[g, :, h].reshape(128, half)
            total += jnp.dot(lhs, wout[h * half : (h + 1) * half, :], preferred_element_type=F32)
        po[128 * g : 128 * g + 128, :] = total

    def share(k, core):
        first = po[pl.ds(pl.multiple_of(24 * k + 8 * core, 8), 8), :]
        return jnp.concatenate([first, po[pl.ds(pl.multiple_of(24 * k + 16, 8), 8), :]], axis=0)

    def d_sibling(g):
        part = pl.ds(D_CUTS[g], D_CUTS[g + 1] - D_CUTS[g])
        return remote(ss.at[part], sr.at[part], ds_send.at[g], ds_recv.at[g], sibling)

    def d_sibling_start(g):
        for k in range(D_CUTS[g], D_CUTS[g + 1]):
            ss[k] = share(k, 1 - c).astype(BF16)
        start(d_sibling(g))

    def chip(k):
        return share(k, c) + sr[k].astype(F32)

    def d_copy(side, m):
        sign = 1 - 2 * side
        place = BASE[m] + side
        return remote(
            zs.at[place], zr.at[place], d_send.at[side, m], d_recv.at[side, m], z_peer(sign * (m - PARENT[m]))
        )

    def d_copy8():
        return remote(zs.at[15], zr.at[15], d_send.at[0, 8], d_recv.at[0, 8], z_peer(4 * s8))

    def d_send_on(side, m, below=()):
        place = BASE[m] + side
        total = chip(place)
        for n in below:
            if n == 8:
                d_copy8().wait_recv()
                total += zr[15].astype(F32)
            else:
                d_copy(side, n).wait_recv()
                total += zr[BASE[n] + side].astype(F32)
        zs[place] = total.astype(BF16)
        start(d_copy(side, m))

    for m in (4, 2, 1):
        for side in (0, 1):
            start(a_copy(side, m, 0))
    for m in (2,):
        for side in (0, 1):
            a_wait(side, m)
            start(a_copy(side, 3, slot(side, 2)))
    for side in (0, 1):
        a_wait(side, 1)
    for side in (0, 1):
        a_wait(side, 4)
        start(a_copy(side, 6, slot(side, 4)))
        start(a_copy(side, 5, slot(side, 4)))
    start(a_copy8())
    start(a_sibling(0))
    a_sibling_wait(0)
    assemble(0)
    load_in.wait()
    project_in(0)
    b_start(0)
    for side in (0, 1):
        a_wait(side, 6)
        start(a_copy(side, 7, slot(side, 6)))
    for side in (0, 1):
        a_wait(side, 5)
        a_wait(side, 3)
    start(a_sibling(1))
    a_sibling_wait(1)
    assemble(1)
    project_in(1)
    b_start(1)
    for side in (0, 1):
        a_wait(side, 7)
    a_copy8().wait_recv()
    start(a_sibling(2))
    b_finish(0)
    c_start(0)
    a_sibling_wait(2)
    assemble(2)
    project_in(2)
    b_start(2)
    b_finish(1)
    c_start(1)
    load_out.wait()
    c_wait(0)
    project_out(0)
    d_sibling_start(0)
    b_finish(2)
    c_start(2)
    d_sibling(0).wait_recv()
    for side in (0, 1):
        d_send_on(side, 1)
    c_wait(1)
    project_out(1)
    d_sibling_start(1)
    d_sibling(1).wait_recv()
    for side in (0, 1):
        d_send_on(side, 3)
    d_send_on(0, 5)
    for side in (0, 1):
        d_send_on(side, 2, (3,))
    c_wait(2)
    project_out(2)
    d_sibling_start(2)
    d_sibling(2).wait_recv()
    for side in (0, 1):
        d_send_on(side, 7)
    zs[15] = chip(15).astype(BF16)
    start(d_copy8())
    d_send_on(1, 5)
    for side in (0, 1):
        d_send_on(side, 6, (7,))
    d_send_on(1 - c, 4, (5, 6))
    d_send_on(c, 4, (5, 6, 8))
    total = chip(0)
    for m in (1, 2, 4):
        for side in (0, 1):
            d_copy(side, m).wait_recv()
            total += zr[BASE[m] + side].astype(F32)
    last = jnp.where(c == 0, total[8:12], total[12:16])
    out = jnp.concatenate([total[0:8], last], axis=0) + bout_ref[...]
    o_ref[...] = out.astype(BF16)
    for copy in sent:
        copy.wait_send()


def on_device(tokens, w_in, b_in, w_out, b_out):
    width, hidden = w_in.shape
    half = hidden // 2
    vmem = pl.BlockSpec(memory_space=pltpu.VMEM)
    hbm = pl.BlockSpec(memory_space=pl.ANY)
    dma = pltpu.SemaphoreType.DMA
    return pl.pallas_call(
        kernel,
        out_shape=jax.ShapeDtypeStruct(tokens.shape, BF16),
        in_specs=[vmem, hbm, vmem, hbm, vmem],
        out_specs=vmem,
        scratch_shapes=[
            pltpu.VMEM((width, hidden), BF16),
            pltpu.VMEM((hidden, width), BF16),
            pltpu.VMEM((2, 16, 16, width), BF16),
            pltpu.VMEM((384, width), BF16),
            pltpu.VMEM((GROUPS, 8, 2, 16, half), F32),
            pltpu.VMEM((GROUPS, 8, 2, 16, half), BF16),
            pltpu.VMEM((GROUPS, 16, 16, half), BF16),
            pltpu.VMEM((GROUPS, 8, 2, 16, half), BF16),
            pltpu.VMEM((384, width), F32),
            pltpu.VMEM((16, 16, width), BF16),
            pltpu.VMEM((16, 16, width), BF16),
            pltpu.VMEM((16, 16, width), BF16),
            pltpu.VMEM((16, 16, width), BF16),
            dma((2,)),
            dma((2, 9)), dma((2, 9)),
            dma((GROUPS,)), dma((GROUPS,)),
            dma((GROUPS, 16)), dma((GROUPS, 16)),
            dma((GROUPS, 16)), dma((GROUPS, 16)),
            dma((GROUPS,)), dma((GROUPS,)),
            dma((2, 9)), dma((2, 9)),
        ],
        compiler_params=pltpu.CompilerParams(
            collective_id=0, has_side_effects=True, vmem_limit_bytes=40 * 2**20
        ),
        cost_estimate=pl.CostEstimate(
            flops=4 * 384 * width * hidden, bytes_accessed=4 * width * hidden, transcendentals=384 * hidden // 16
        ),
    )(tokens, w_in, b_in.reshape(1, -1), w_out, b_out.reshape(1, -1))


def solution(mesh):
    return jax.shard_map(
        on_device,
        mesh=mesh,
        in_specs=(P("row", "col"), P("col", "row"), P("row"), P("row", "col"), P("col")),
        out_specs=P("row", "col"),
        check_vma=False,
    )
```

```python
import functools

import jax
import jax.numpy as jnp
from jax import lax
from jax.experimental import pallas as pl
from jax.experimental.pallas import tpu as pltpu
from jax.sharding import PartitionSpec as P

BF16 = jnp.bfloat16
F32 = jnp.float32
PARENT = {1: 0, 2: 0, 5: 0, 3: 2, 4: 5, 6: 5, 7: 5, 8: 5}
OWN = 15
PLANE = [(dy, dx) for dy in (2, 1, 3, 0) for dx in (2, 1, 3, 0) if (dy, dx) != (0, 0)]
GROUPS = 3
A_CUTS = (0, 6, 10, 16)
D_CUTS = (0, 5, 10, 16)


def slot(side, m):
    if m == 3:
        return 10 - side
    return {8: 0, 7: 1, 6: 3, 4: 5, 5: 7, 2: 11, 1: 13}[m] + side


def parent_out(side, m):
    return 0 if m == 3 and side == 0 else PARENT[m]


def kernel(
    tok_hbm, win_ref, bin_hbm, wout_ref, bout_hbm, o_ref,
    tok, win, b_in, wout, b_out, ta, xs, pf, pb, rb, hid, po, ss, sr, zs, zr,
    wsem, a_send, a_recv, as_send, as_recv, b_send, b_recv, c_send, c_recv,
    ds_send, ds_recv, d_send, d_recv,
):
    row, col = lax.axis_index("row"), lax.axis_index("col")
    z, c = row // 2, row % 2
    y, x = col // 4, col % 4
    half = pb.shape[-1]
    s8 = 1 - 2 * c

    def z_peer(dz):
        return {"row": lax.rem(z + dz + 16, 16) * 2 + c, "col": col}

    def plane_col(dy, dx):
        return lax.rem(y + dy + 4, 4) * 4 + lax.rem(x + dx + 4, 4)

    def plane_peer(dy, dx):
        return {"row": row, "col": plane_col(dy, dx)}

    sibling = {"row": z * 2 + (1 - c), "col": col}

    def remote(src, dst, send, recv, peer):
        return pltpu.make_async_remote_copy(
            src_ref=src, dst_ref=dst, send_sem=send, recv_sem=recv,
            device_id=peer, device_id_type=pl.DeviceIdType.MESH,
        )

    def start(copy):
        copy.start()

    def all_of(block, send, recv):
        return remote(block, block, send, recv, sibling)

    load_tok = pltpu.make_async_copy(tok_hbm, tok, wsem.at[2])
    load_tok.start()

    barrier = pltpu.get_barrier_semaphore()
    peers = [z_peer(dz) for dz in (5, -5, 3, -3, 2, -2, 1, -1)]
    peers += [plane_peer(dy, dx) for dy, dx in PLANE] + [sibling]
    for peer in peers:
        pl.semaphore_signal(barrier, inc=1, device_id=peer, device_id_type=pl.DeviceIdType.MESH)
    load_in = pltpu.make_async_copy(win_ref, win, wsem.at[0])
    load_out = pltpu.make_async_copy(wout_ref, wout, wsem.at[1])
    load_b_in = pltpu.make_async_copy(bin_hbm, b_in, wsem.at[3])
    load_b_out = pltpu.make_async_copy(bout_hbm, b_out, wsem.at[4])
    for load in (load_in, load_out, load_b_in, load_b_out):
        load.start()
    load_tok.wait()

    own = tok[...].astype(F32)
    tail, none = own[8:12], jnp.zeros((4, own.shape[1]), F32)
    tail = jnp.where(
        c == 0, jnp.concatenate([tail, none], axis=0), jnp.concatenate([none, tail], axis=0)
    )
    ta[c, OWN] = jnp.concatenate([own[0:8], tail], axis=0).astype(BF16)
    pl.semaphore_wait(barrier, len(peers))

    def a_copy(side, m, at):
        sign = 1 - 2 * side
        dz = -sign * (m - PARENT[m])
        place = slot(side, m)
        return remote(ta.at[c, at], ta.at[c, place], a_send.at[0], a_recv.at[side, m], z_peer(dz))

    def a_copy8():
        return remote(ta.at[c, slot(0, 5) + c], ta.at[c, 0], a_send.at[0], a_recv.at[0, 8], z_peer(-3 * s8))

    def a_wait(side, m):
        a_copy(side, m, 0).wait_recv()

    def a_sibling(g, place):
        start(remote(ta.at[c, place], ta.at[c, place], as_send.at[0], as_recv.at[g], sibling))

    def a_sibling_wait(g):
        part = pl.ds(A_CUTS[g], A_CUTS[g + 1] - A_CUTS[g])
        all_of(ta.at[1 - c, part], as_send.at[0], as_recv.at[g]).wait_recv()

    def a_take(side, m):
        a_wait(side, m)
        place = slot(side, m)
        a_sibling(sum(place >= cut for cut in A_CUTS[1:]), place)

    def a_sent():
        all_of(ta.at[c, pl.ds(0, 15)], a_send.at[0], as_recv.at[0]).wait_send()
        all_of(ta.at[c], as_send.at[0], as_recv.at[0]).wait_send()

    def assemble(g):
        for k in range(A_CUTS[g], A_CUTS[g + 1], 2):
            rows = []
            for i in (k, k + 1):
                first, second = ta[0, i].astype(F32), ta[1, i].astype(F32)
                rows += [first[0:8], second[0:8], first[8:16] + second[8:16]]
            xs[24 * k : 24 * k + 48, :] = jnp.concatenate(rows, axis=0).astype(BF16)

    def project_in(g):
        lhs = xs[128 * g : 128 * g + 128, :]

        @pl.loop(0, 2)
        def _(h):
            cols = pl.ds(pl.multiple_of(h * half, 128), half)
            part = jnp.dot(lhs, win[:, cols], preferred_element_type=F32).reshape(8, 16, half)
            pf[g, :, h] = part
            pb[g, :, h] = part.astype(BF16)

    def b_copy(g, dy, dx):
        there = plane_col(dy, dx)
        d = dy * 4 + dx
        return remote(
            pb.at[g, there // 2, there % 2], rb.at[g, d], b_send.at[g], b_recv.at[g], plane_peer(dy, dx)
        )

    def b_start(g):
        for dy, dx in PLANE:
            start(b_copy(g, dy, dx))

    def b_finish(g):
        total = pf[g, col // 2, col % 2]
        blocks = all_of(rb.at[g, pl.ds(1, 15)], b_send.at[g], b_recv.at[g])
        blocks.wait_recv()
        for dy, dx in PLANE:
            total += rb[g, dy * 4 + dx].astype(F32)
        v = total + b_in[pl.ds(pl.multiple_of((col % 2) * half, 128), half)].reshape(1, half)
        v = 0.5 * v * (1.0 + jnp.tanh(0.7978845608 * (v + 0.044715 * (v * v * v))))
        hid[g, col // 2, col % 2] = v.astype(BF16)

    def c_start(g):
        block = hid.at[g, col // 2, col % 2]
        for dy, dx in PLANE:
            start(remote(block, block, c_send.at[g], c_recv.at[g], plane_peer(dy, dx)))

    def c_wait(g):
        all_of(rb.at[g, pl.ds(1, 15)], c_send.at[g], c_recv.at[g]).wait_recv()

    def plane_sent(g):
        all_of(rb.at[g, pl.ds(1, 15)], b_send.at[g], b_recv.at[g]).wait_send()
        all_of(rb.at[g, pl.ds(1, 15)], c_send.at[g], c_recv.at[g]).wait_send()

    def project_out(g):
        total = jnp.zeros((128, po.shape[1]), F32)
        for h in range(2):
            lhs = hid[g, :, h].reshape(128, half)
            total += jnp.dot(lhs, wout[h * half : (h + 1) * half, :], preferred_element_type=F32)
        po[128 * g : 128 * g + 128, :] = total

    def share(k, core):
        first = po[pl.ds(pl.multiple_of(24 * k + 8 * core, 8), 8), :]
        return jnp.concatenate([first, po[pl.ds(pl.multiple_of(24 * k + 16, 8), 8), :]], axis=0)

    def d_sibling(g):
        part = pl.ds(D_CUTS[g], D_CUTS[g + 1] - D_CUTS[g])
        return remote(ss.at[part], sr.at[part], ds_send.at[0], ds_recv.at[g], sibling)

    def d_sibling_start(g):
        for k in range(D_CUTS[g], D_CUTS[g + 1]):
            ss[k] = share(k, 1 - c).astype(BF16)
        start(d_sibling(g))

    def chip(k):
        return share(k, c) + sr[k].astype(F32)

    def d_copy(side, m):
        dz = (1 - 2 * side) * (m - parent_out(side, m))
        place = slot(side, m)
        return remote(zs.at[place], zr.at[place], d_send.at[0], d_recv.at[side, m], z_peer(dz))

    def d_copy8():
        return remote(zs.at[0], zr.at[0], d_send.at[0], d_recv.at[0, 8], z_peer(3 * s8))

    def d_sent():
        all_of(sr, ds_send.at[0], ds_recv.at[0]).wait_send()
        all_of(zr.at[pl.ds(0, 15)], d_send.at[0], ds_recv.at[0]).wait_send()

    def d_send_on(side, m, below=()):
        place = slot(side, m)
        total = chip(place)
        for n in below:
            if n == 8:
                d_copy8().wait_recv()
                total += zr[0].astype(F32)
            else:
                d_copy(side, n).wait_recv()
                total += zr[slot(side, n)].astype(F32)
        zs[place] = total.astype(BF16)
        start(d_copy(side, m))

    for m in (5, 2, 1):
        for side in (0, 1):
            start(a_copy(side, m, OWN))
    a_sibling(2, OWN)
    for side in (0, 1):
        a_take(side, 2)
        start(a_copy(side, 3, slot(side, 2)))
    for side in (0, 1):
        a_take(side, 1)
    for side in (0, 1):
        a_take(side, 5)
        for m in (7, 6, 4):
            start(a_copy(side, m, slot(side, 5)))
    start(a_copy8())
    a_take(0, 3)
    load_in.wait()
    load_b_in.wait()
    load_b_out.wait()
    a_sibling_wait(2)
    assemble(2)
    project_in(2)
    b_start(2)
    for m in (6, 7):
        for side in (0, 1):
            a_take(side, m)
    a_copy8().wait_recv()
    a_sibling(0, 0)
    a_take(0, 4)
    a_take(1, 4)
    a_take(1, 3)
    a_sibling_wait(0)
    assemble(0)
    project_in(0)
    b_start(0)
    a_sibling_wait(1)
    assemble(1)
    project_in(1)
    b_start(1)
    load_out.wait()
    b_finish(2)
    b_finish(0)
    c_start(0)
    a_sent()
    b_finish(1)
    c_start(1)
    c_start(2)
    c_wait(0)
    project_out(0)
    d_sibling_start(0)
    d_sibling(0).wait_recv()
    zs[0] = chip(0).astype(BF16)
    start(d_copy8())
    for m in (7, 6):
        for side in (0, 1):
            d_send_on(side, m)
    c_wait(1)
    project_out(1)
    d_sibling_start(1)
    d_sibling(1).wait_recv()
    for side in (0, 1):
        d_send_on(side, 4)
    d_send_on(1, 3)
    c_wait(2)
    project_out(2)
    d_sibling_start(2)
    d_send_on(1 - c, 5, (4, 6, 7))
    d_send_on(c, 5, (4, 6, 7, 8))
    d_sibling(2).wait_recv()
    d_send_on(0, 3)
    d_send_on(0, 2)
    d_send_on(1, 2, (3,))
    for side in (0, 1):
        d_send_on(side, 1)
    for g in range(GROUPS):
        plane_sent(g)
    total = chip(OWN)
    for side, m in ((0, 1), (1, 1), (0, 2), (1, 2), (0, 3), (0, 5), (1, 5)):
        d_copy(side, m).wait_recv()
        total += zr[slot(side, m)].astype(F32)
    last = jnp.where(c == 0, total[8:12], total[12:16])
    out = jnp.concatenate([total[0:8], last], axis=0) + b_out[...].reshape(1, -1)
    o_ref[...] = out.astype(BF16)
    d_sent()


def on_device(tokens, w_in, b_in, w_out, b_out):
    width, hidden = w_in.shape
    half = hidden // 2
    vmem = pl.BlockSpec(memory_space=pltpu.VMEM)
    hbm = pl.BlockSpec(memory_space=pltpu.HBM)
    dma = pltpu.SemaphoreType.DMA
    return pl.pallas_call(
        kernel,
        out_shape=jax.ShapeDtypeStruct(tokens.shape, BF16),
        in_specs=[hbm] * 5,
        out_specs=vmem,
        scratch_shapes=[
            pltpu.VMEM(tokens.shape, BF16),
            pltpu.VMEM((width, hidden), BF16),
            pltpu.VMEM(b_in.shape, F32),
            pltpu.VMEM((hidden, width), BF16),
            pltpu.VMEM(b_out.shape, F32),
            pltpu.VMEM((2, 16, 16, width), BF16),
            pltpu.VMEM((384, width), BF16),
            pltpu.VMEM((GROUPS, 8, 2, 16, half), F32),
            pltpu.VMEM((GROUPS, 8, 2, 16, half), BF16),
            pltpu.VMEM((GROUPS, 16, 16, half), BF16),
            pltpu.VMEM((GROUPS, 8, 2, 16, half), BF16),
            pltpu.VMEM((384, width), F32),
            pltpu.VMEM((16, 16, width), BF16),
            pltpu.VMEM((16, 16, width), BF16),
            pltpu.VMEM((16, 16, width), BF16),
            pltpu.VMEM((16, 16, width), BF16),
            dma((5,)),
            dma((1,)), dma((2, 9)),
            dma((1,)), dma((GROUPS,)),
            dma((GROUPS,)), dma((GROUPS,)),
            dma((GROUPS,)), dma((GROUPS,)),
            dma((1,)), dma((GROUPS,)),
            dma((1,)), dma((2, 9)),
        ],
        compiler_params=pltpu.CompilerParams(
            collective_id=0, has_side_effects=True, vmem_limit_bytes=60 * 2**20
        ),
        cost_estimate=pl.CostEstimate(
            flops=4 * 384 * width * hidden, bytes_accessed=4 * width * hidden, transcendentals=384 * hidden // 16
        ),
    )(tokens, w_in, b_in, w_out, b_out)


def solution(mesh):
    return jax.shard_map(
        on_device,
        mesh=mesh,
        in_specs=(P("row", "col"), P("col", "row"), P("row"), P("row", "col"), P("col")),
        out_specs=P("row", "col"),
        check_vma=False,
    )
```

```python
import functools

import jax
import jax.numpy as jnp
from jax import lax
from jax.experimental import pallas as pl
from jax.experimental.pallas import tpu as pltpu
from jax.sharding import PartitionSpec as P

BF16 = jnp.bfloat16
F32 = jnp.float32
PARENT = {1: 0, 2: 0, 5: 0, 3: 2, 4: 5, 6: 5, 7: 5, 8: 5}
PARENT_OUT = {1: 0, 2: 0, 3: 0, 4: 0, 5: 0, 6: 5, 7: 5, 8: 5}
OWN = 9
PLANE = [(dy, dx) for dy in (2, 1, 3, 0) for dx in (2, 1, 3, 0) if (dy, dx) != (0, 0)]
GROUPS = 3
A_CUTS = (0, 6, 10, 16)
D_CUTS = (0, 5, 11, 16)


def slot(side, m):
    if m == 2:
        return 11 - side
    return {8: 0, 7: 1, 6: 3, 4: 5, 3: 7, 1: 12, 5: 14}[m] + side


def kernel(
    tok_hbm, win_ref, bin_hbm, wout_ref, bout_hbm, o_ref,
    tok, win, b_in, wout, b_out, ta, xs, pf, pb, rb, hid, po, ss, sr, zs, zr,
    wsem, a_send, a_recv, as_send, as_recv, b_send, b_recv, c_send, c_recv,
    ds_send, ds_recv, d_send, d_recv,
):
    row, col = lax.axis_index("row"), lax.axis_index("col")
    z, c = row // 2, row % 2
    y, x = col // 4, col % 4
    half = pb.shape[-1]
    s8 = 1 - 2 * c

    def z_peer(dz):
        return {"row": lax.rem(z + dz + 16, 16) * 2 + c, "col": col}

    def plane_col(dy, dx):
        return lax.rem(y + dy + 4, 4) * 4 + lax.rem(x + dx + 4, 4)

    def plane_peer(dy, dx):
        return {"row": row, "col": plane_col(dy, dx)}

    sibling = {"row": z * 2 + (1 - c), "col": col}

    def remote(src, dst, send, recv, peer):
        return pltpu.make_async_remote_copy(
            src_ref=src, dst_ref=dst, send_sem=send, recv_sem=recv,
            device_id=peer, device_id_type=pl.DeviceIdType.MESH,
        )

    def start(copy):
        copy.start()

    def all_of(block, send, recv):
        return remote(block, block, send, recv, sibling)

    load_tok = pltpu.make_async_copy(tok_hbm, tok, wsem.at[2])
    load_tok.start()

    barrier = pltpu.get_barrier_semaphore()
    peers = [z_peer(dz) for dz in (5, -5, 4, -4, 3, -3, 2, -2, 1, -1)]
    peers += [plane_peer(dy, dx) for dy, dx in PLANE] + [sibling]
    for peer in peers:
        pl.semaphore_signal(barrier, inc=1, device_id=peer, device_id_type=pl.DeviceIdType.MESH)
    load_in = pltpu.make_async_copy(win_ref, win, wsem.at[0])
    load_out = pltpu.make_async_copy(wout_ref, wout, wsem.at[1])
    load_b_in = pltpu.make_async_copy(bin_hbm, b_in, wsem.at[3])
    load_b_out = pltpu.make_async_copy(bout_hbm, b_out, wsem.at[4])
    for load in (load_in, load_out, load_b_in, load_b_out):
        load.start()
    load_tok.wait()

    own = tok[...].astype(F32)
    tail, none = own[8:12], jnp.zeros((4, own.shape[1]), F32)
    tail = jnp.where(
        c == 0, jnp.concatenate([tail, none], axis=0), jnp.concatenate([none, tail], axis=0)
    )
    ta[c, OWN] = jnp.concatenate([own[0:8], tail], axis=0).astype(BF16)
    pl.semaphore_wait(barrier, len(peers))

    def a_copy(side, m, at):
        sign = 1 - 2 * side
        dz = -sign * (m - PARENT[m])
        place = slot(side, m)
        return remote(ta.at[c, at], ta.at[c, place], a_send.at[0], a_recv.at[side, m], z_peer(dz))

    def a_copy8():
        return remote(ta.at[c, slot(0, 5) + c], ta.at[c, 0], a_send.at[0], a_recv.at[0, 8], z_peer(-3 * s8))

    def a_wait(side, m):
        a_copy(side, m, 0).wait_recv()

    def a_sibling(g, place):
        start(remote(ta.at[c, place], ta.at[c, place], as_send.at[0], as_recv.at[g], sibling))

    def a_sibling_wait(g):
        part = pl.ds(A_CUTS[g], A_CUTS[g + 1] - A_CUTS[g])
        all_of(ta.at[1 - c, part], as_send.at[0], as_recv.at[g]).wait_recv()

    def a_take(side, m):
        a_wait(side, m)
        place = slot(side, m)
        a_sibling(sum(place >= cut for cut in A_CUTS[1:]), place)

    def a_sent():
        all_of(ta.at[c, pl.ds(0, 15)], a_send.at[0], as_recv.at[0]).wait_send()
        all_of(ta.at[c], as_send.at[0], as_recv.at[0]).wait_send()

    def assemble(g):
        for k in range(A_CUTS[g], A_CUTS[g + 1], 2):
            rows = []
            for i in (k, k + 1):
                first, second = ta[0, i].astype(F32), ta[1, i].astype(F32)
                rows += [first[0:8], second[0:8], first[8:16] + second[8:16]]
            xs[24 * k : 24 * k + 48, :] = jnp.concatenate(rows, axis=0).astype(BF16)

    def project_in(g):
        lhs = xs[128 * g : 128 * g + 128, :]

        @pl.loop(0, 2)
        def _(h):
            cols = pl.ds(pl.multiple_of(h * half, 128), half)
            part = jnp.dot(lhs, win[:, cols], preferred_element_type=F32).reshape(8, 16, half)
            pf[g, :, h] = part
            pb[g, :, h] = part.astype(BF16)

    def b_copy(g, dy, dx):
        there = plane_col(dy, dx)
        d = dy * 4 + dx
        return remote(
            pb.at[g, there // 2, there % 2], rb.at[g, d], b_send.at[g], b_recv.at[g], plane_peer(dy, dx)
        )

    def b_start(g):
        for dy, dx in PLANE:
            start(b_copy(g, dy, dx))

    def b_finish(g):
        total = pf[g, col // 2, col % 2]
        blocks = all_of(rb.at[g, pl.ds(1, 15)], b_send.at[g], b_recv.at[g])
        blocks.wait_recv()
        for dy, dx in PLANE:
            total += rb[g, dy * 4 + dx].astype(F32)
        v = total + b_in[pl.ds(pl.multiple_of((col % 2) * half, 128), half)].reshape(1, half)
        v = 0.5 * v * (1.0 + jnp.tanh(0.7978845608 * (v + 0.044715 * (v * v * v))))
        hid[g, col // 2, col % 2] = v.astype(BF16)

    def c_start(g):
        block = hid.at[g, col // 2, col % 2]
        for dy, dx in PLANE:
            start(remote(block, block, c_send.at[g], c_recv.at[g], plane_peer(dy, dx)))

    def c_wait(g):
        all_of(rb.at[g, pl.ds(1, 15)], c_send.at[g], c_recv.at[g]).wait_recv()

    def plane_sent(g):
        all_of(rb.at[g, pl.ds(1, 15)], b_send.at[g], b_recv.at[g]).wait_send()
        all_of(rb.at[g, pl.ds(1, 15)], c_send.at[g], c_recv.at[g]).wait_send()

    def project_out(g):
        total = jnp.zeros((128, po.shape[1]), F32)
        for h in range(2):
            lhs = hid[g, :, h].reshape(128, half)
            total += jnp.dot(lhs, wout[h * half : (h + 1) * half, :], preferred_element_type=F32)
        po[128 * g : 128 * g + 128, :] = total

    def share(k, core):
        first = po[pl.ds(pl.multiple_of(24 * k + 8 * core, 8), 8), :]
        return jnp.concatenate([first, po[pl.ds(pl.multiple_of(24 * k + 16, 8), 8), :]], axis=0)

    def d_sibling(g):
        part = pl.ds(D_CUTS[g], D_CUTS[g + 1] - D_CUTS[g])
        return remote(ss.at[part], sr.at[part], ds_send.at[0], ds_recv.at[g], sibling)

    def d_sibling_start(g):
        for k in range(D_CUTS[g], D_CUTS[g + 1]):
            ss[k] = share(k, 1 - c).astype(BF16)
        start(d_sibling(g))

    def chip(k):
        return share(k, c) + sr[k].astype(F32)

    def d_copy(side, m):
        dz = (1 - 2 * side) * (m - PARENT_OUT[m])
        place = slot(side, m)
        return remote(zs.at[place], zr.at[place], d_send.at[0], d_recv.at[side, m], z_peer(dz))

    def d_copy8():
        return remote(zs.at[0], zr.at[0], d_send.at[0], d_recv.at[0, 8], z_peer(3 * s8))

    def d_sent():
        all_of(sr, ds_send.at[0], ds_recv.at[0]).wait_send()
        all_of(zr.at[pl.ds(0, 15)], d_send.at[0], ds_recv.at[0]).wait_send()

    def d_send_on(side, m, below=()):
        place = slot(side, m)
        total = chip(place)
        for n in below:
            if n == 8:
                d_copy8().wait_recv()
                total += zr[0].astype(F32)
            else:
                d_copy(side, n).wait_recv()
                total += zr[slot(side, n)].astype(F32)
        zs[place] = total.astype(BF16)
        start(d_copy(side, m))

    for m in (5, 2, 1):
        for side in (0, 1):
            start(a_copy(side, m, OWN))
    a_sibling(1, OWN)
    for side in (0, 1):
        a_take(side, 2)
        start(a_copy(side, 3, slot(side, 2)))
    for side in (0, 1):
        a_take(side, 1)
    for side in (0, 1):
        a_take(side, 5)
        for m in (7, 6, 4):
            start(a_copy(side, m, slot(side, 5)))
    start(a_copy8())
    load_in.wait()
    load_b_in.wait()
    load_b_out.wait()
    a_sibling_wait(2)
    assemble(2)
    project_in(2)
    b_start(2)
    for m in (3, 6, 7):
        for side in (0, 1):
            a_take(side, m)
    a_copy8().wait_recv()
    a_sibling(0, 0)
    for side in (0, 1):
        a_take(side, 4)
    b_finish(2)
    c_start(2)
    a_sibling_wait(0)
    assemble(0)
    project_in(0)
    b_start(0)
    a_sibling_wait(1)
    assemble(1)
    project_in(1)
    b_start(1)
    load_out.wait()
    a_sent()
    c_wait(2)
    project_out(2)
    d_sibling_start(2)
    b_finish(0)
    c_start(0)
    d_sibling(2).wait_recv()
    for side in (0, 1):
        d_send_on(side, 1)
    d_send_on(0, 2)
    b_finish(1)
    c_start(1)
    c_wait(0)
    project_out(0)
    d_sibling_start(0)
    d_sibling(0).wait_recv()
    zs[0] = chip(0).astype(BF16)
    start(d_copy8())
    for m in (7, 6):
        for side in (0, 1):
            d_send_on(side, m)
    c_wait(1)
    project_out(1)
    d_sibling_start(1)
    for g in range(GROUPS):
        plane_sent(g)
    d_sibling(1).wait_recv()
    for m in (4, 3):
        for side in (0, 1):
            d_send_on(side, m)
    d_send_on(1, 2)
    d_send_on(1 - c, 5, (6, 7))
    d_send_on(c, 5, (6, 7, 8))
    total = chip(OWN)
    for m in (1, 2, 3, 4, 5):
        for side in (0, 1):
            d_copy(side, m).wait_recv()
            total += zr[slot(side, m)].astype(F32)
    last = jnp.where(c == 0, total[8:12], total[12:16])
    out = jnp.concatenate([total[0:8], last], axis=0) + b_out[...].reshape(1, -1)
    o_ref[...] = out.astype(BF16)
    d_sent()


def on_device(tokens, w_in, b_in, w_out, b_out):
    width, hidden = w_in.shape
    half = hidden // 2
    vmem = pl.BlockSpec(memory_space=pltpu.VMEM)
    hbm = pl.BlockSpec(memory_space=pltpu.HBM)
    dma = pltpu.SemaphoreType.DMA
    return pl.pallas_call(
        kernel,
        out_shape=jax.ShapeDtypeStruct(tokens.shape, BF16),
        in_specs=[hbm] * 5,
        out_specs=vmem,
        scratch_shapes=[
            pltpu.VMEM(tokens.shape, BF16),
            pltpu.VMEM((width, hidden), BF16),
            pltpu.VMEM(b_in.shape, F32),
            pltpu.VMEM((hidden, width), BF16),
            pltpu.VMEM(b_out.shape, F32),
            pltpu.VMEM((2, 16, 16, width), BF16),
            pltpu.VMEM((384, width), BF16),
            pltpu.VMEM((GROUPS, 8, 2, 16, half), F32),
            pltpu.VMEM((GROUPS, 8, 2, 16, half), BF16),
            pltpu.VMEM((GROUPS, 16, 16, half), BF16),
            pltpu.VMEM((GROUPS, 8, 2, 16, half), BF16),
            pltpu.VMEM((384, width), F32),
            pltpu.VMEM((16, 16, width), BF16),
            pltpu.VMEM((16, 16, width), BF16),
            pltpu.VMEM((16, 16, width), BF16),
            pltpu.VMEM((16, 16, width), BF16),
            dma((5,)),
            dma((1,)), dma((2, 9)),
            dma((1,)), dma((GROUPS,)),
            dma((GROUPS,)), dma((GROUPS,)),
            dma((GROUPS,)), dma((GROUPS,)),
            dma((1,)), dma((GROUPS,)),
            dma((1,)), dma((2, 9)),
        ],
        compiler_params=pltpu.CompilerParams(
            collective_id=0, has_side_effects=True, vmem_limit_bytes=60 * 2**20
        ),
        cost_estimate=pl.CostEstimate(
            flops=4 * 384 * width * hidden, bytes_accessed=4 * width * hidden, transcendentals=384 * hidden // 16
        ),
    )(tokens, w_in, b_in, w_out, b_out)


def solution(mesh):
    return jax.shard_map(
        on_device,
        mesh=mesh,
        in_specs=(P("row", "col"), P("col", "row"), P("row"), P("row", "col"), P("col")),
        out_specs=P("row", "col"),
        check_vma=False,
    )
```

```python
import functools

import jax
import jax.numpy as jnp
from jax import lax
from jax.experimental import pallas as pl
from jax.experimental.pallas import tpu as pltpu
from jax.sharding import PartitionSpec as P

BF16 = jnp.bfloat16
F32 = jnp.float32
PARENT = {1: 0, 2: 0, 5: 0, 3: 2, 4: 5, 6: 5, 7: 5, 8: 5}
PARENT_OUT = {1: 0, 2: 0, 3: 0, 4: 0, 5: 0, 6: 5, 7: 5, 8: 5}
SPLIT, OWN = 10, 11
PLANE = [(dy, dx) for dy in (2, 1, 3, 0) for dx in (2, 1, 3, 0) if (dy, dx) != (0, 0)]
GROUPS = 3
CHUNKS = ((0, 5), (5, 10), (11, 16))
PARTS = ((0, 5), (5, 10), (10, 16))


def slot(side, m):
    if m == 3:
        return (2, SPLIT)[side]
    return {5: 0, 4: 3, 8: 5, 7: 6, 6: 8, 1: 12, 2: 14}[m] + side


def first_row(place):
    if not isinstance(place, int):
        return 24 * place
    group = 0 if place < 5 else 1 if place < 10 else 2
    return 128 * group + 24 * (place - CHUNKS[group][0])


def kernel(
    tok_hbm, win_ref, bin_hbm, wout_ref, bout_hbm, o_ref,
    tok, win, b_in, wout, b_out, ta, xs, pf, pb, rb, hid, po, ss, sr, zs, zr,
    wsem, a_send, a_recv, as_send, as_recv, b_send, b_recv, c_send, c_recv,
    ds_send, ds_recv, d_send, d_recv,
):
    row, col = lax.axis_index("row"), lax.axis_index("col")
    z, c = row // 2, row % 2
    y, x = col // 4, col % 4
    half = pb.shape[-1]
    s8 = 1 - 2 * c

    def z_peer(dz):
        return {"row": lax.rem(z + dz + 16, 16) * 2 + c, "col": col}

    def plane_col(dy, dx):
        return lax.rem(y + dy + 4, 4) * 4 + lax.rem(x + dx + 4, 4)

    def plane_peer(dy, dx):
        return {"row": row, "col": plane_col(dy, dx)}

    sibling = {"row": z * 2 + (1 - c), "col": col}

    def remote(src, dst, send, recv, peer):
        return pltpu.make_async_remote_copy(
            src_ref=src, dst_ref=dst, send_sem=send, recv_sem=recv,
            device_id=peer, device_id_type=pl.DeviceIdType.MESH,
        )

    def start(copy):
        copy.start()

    def all_of(block, send, recv):
        return remote(block, block, send, recv, sibling)

    load_tok = pltpu.make_async_copy(tok_hbm, tok, wsem.at[2])
    load_tok.start()

    barrier = pltpu.get_barrier_semaphore()
    peers = [z_peer(dz) for dz in (5, -5, 4, -4, 3, -3, 2, -2, 1, -1)]
    peers += [plane_peer(dy, dx) for dy, dx in PLANE] + [sibling]
    for peer in peers:
        pl.semaphore_signal(barrier, inc=1, device_id=peer, device_id_type=pl.DeviceIdType.MESH)
    load_in = pltpu.make_async_copy(win_ref, win, wsem.at[0])
    load_out = pltpu.make_async_copy(wout_ref, wout, wsem.at[1])
    load_b_in = pltpu.make_async_copy(bin_hbm, b_in, wsem.at[3])
    load_b_out = pltpu.make_async_copy(bout_hbm, b_out, wsem.at[4])
    for load in (load_in, load_out, load_b_in, load_b_out):
        load.start()
    load_tok.wait()

    own = tok[...].astype(F32)
    tail, none = own[8:12], jnp.zeros((4, own.shape[1]), F32)
    tail = jnp.where(
        c == 0, jnp.concatenate([tail, none], axis=0), jnp.concatenate([none, tail], axis=0)
    )
    ta[c, OWN] = jnp.concatenate([own[0:8], tail], axis=0).astype(BF16)
    pl.semaphore_wait(barrier, len(peers))

    def a_copy(side, m, at):
        sign = 1 - 2 * side
        dz = -sign * (m - (0 if m == 3 and side == 1 else PARENT[m]))
        place = slot(side, m)
        return remote(ta.at[c, at], ta.at[c, place], a_send.at[0], a_recv.at[side, m], z_peer(dz))

    def a_copy8():
        return remote(ta.at[c, slot(0, 5) + c], ta.at[c, slot(0, 8)], a_send.at[0], a_recv.at[0, 8], z_peer(-3 * s8))

    def a_wait(side, m):
        a_copy(side, m, 0).wait_recv()

    def a_sibling(g, place):
        start(remote(ta.at[c, place], ta.at[c, place], as_send.at[0], as_recv.at[g], sibling))

    def a_sibling_wait(g):
        part = pl.ds(PARTS[g][0], PARTS[g][1] - PARTS[g][0])
        all_of(ta.at[1 - c, part], as_send.at[0], as_recv.at[g]).wait_recv()

    def a_take(side, m):
        a_wait(side, m)
        place = slot(side, m)
        a_sibling(0 if place < 5 else 1 if place < 10 else 2, place)

    def a_sent():
        all_of(ta.at[c, pl.ds(0, 15)], a_send.at[0], as_recv.at[0]).wait_send()
        all_of(ta.at[c], as_send.at[0], as_recv.at[0]).wait_send()

    def assemble(g):
        rows = []
        for k in range(*CHUNKS[g]):
            first, second = ta[0, k].astype(F32), ta[1, k].astype(F32)
            rows += [first[0:8], second[0:8], first[8:16] + second[8:16]]
        if g < 2:
            rows.append(ta[g, SPLIT].astype(F32)[0:8])
        else:
            rows.append(ta[0, SPLIT].astype(F32)[8:16] + ta[1, SPLIT].astype(F32)[8:16])
        xs[128 * g : 128 * g + 128, :] = jnp.concatenate(rows, axis=0).astype(BF16)

    def project_in(g):
        lhs = xs[128 * g : 128 * g + 128, :]

        @pl.loop(0, 2)
        def _(h):
            cols = pl.ds(pl.multiple_of(h * half, 128), half)
            part = jnp.dot(lhs, win[:, cols], preferred_element_type=F32).reshape(8, 16, half)
            pf[g, :, h] = part
            pb[g, :, h] = part.astype(BF16)

    def b_copy(g, dy, dx):
        there = plane_col(dy, dx)
        d = dy * 4 + dx
        return remote(
            pb.at[g, there // 2, there % 2], rb.at[g, d], b_send.at[g], b_recv.at[g], plane_peer(dy, dx)
        )

    def b_start(g):
        for dy, dx in PLANE:
            start(b_copy(g, dy, dx))

    def b_finish(g):
        total = pf[g, col // 2, col % 2]
        blocks = all_of(rb.at[g, pl.ds(1, 15)], b_send.at[g], b_recv.at[g])
        blocks.wait_recv()
        for dy, dx in PLANE:
            total += rb[g, dy * 4 + dx].astype(F32)
        v = total + b_in[pl.ds(pl.multiple_of((col % 2) * half, 128), half)].reshape(1, half)
        v = 0.5 * v * (1.0 + jnp.tanh(0.7978845608 * (v + 0.044715 * (v * v * v))))
        hid[g, col // 2, col % 2] = v.astype(BF16)

    def c_start(g):
        block = hid.at[g, col // 2, col % 2]
        for dy, dx in PLANE:
            start(remote(block, block, c_send.at[g], c_recv.at[g], plane_peer(dy, dx)))

    def c_wait(g):
        all_of(rb.at[g, pl.ds(1, 15)], c_send.at[g], c_recv.at[g]).wait_recv()

    def plane_sent(g):
        all_of(rb.at[g, pl.ds(1, 15)], b_send.at[g], b_recv.at[g]).wait_send()
        all_of(rb.at[g, pl.ds(1, 15)], c_send.at[g], c_recv.at[g]).wait_send()

    def project_out(g):
        total = jnp.zeros((128, po.shape[1]), F32)
        for h in range(2):
            lhs = hid[g, :, h].reshape(128, half)
            total += jnp.dot(lhs, wout[h * half : (h + 1) * half, :], preferred_element_type=F32)
        po[128 * g : 128 * g + 128, :] = total

    def share(k, core):
        if isinstance(k, int) and k == SPLIT:
            first, rest = 128 * core + 120, 256 + 120
        else:
            first, rest = first_row(k) + 8 * core, first_row(k) + 16
        first, rest = (po[pl.ds(pl.multiple_of(at, 8), 8), :] for at in (first, rest))
        return jnp.concatenate([first, rest], axis=0)

    def d_sibling(g):
        part = pl.ds(PARTS[g][0], PARTS[g][1] - PARTS[g][0])
        return remote(ss.at[part], sr.at[part], ds_send.at[0], ds_recv.at[g], sibling)

    def d_sibling_start(g):
        for k in range(*PARTS[g]):
            ss[k] = share(k, 1 - c).astype(BF16)
        start(d_sibling(g))

    def chip(k):
        return share(k, c) + sr[k].astype(F32)

    def d_copy(side, m):
        dz = (1 - 2 * side) * (m - PARENT_OUT[m])
        place = slot(side, m)
        return remote(zs.at[place], zr.at[place], d_send.at[0], d_recv.at[side, m], z_peer(dz))

    def d_copy8():
        return remote(zs.at[slot(0, 8)], zr.at[slot(0, 8)], d_send.at[0], d_recv.at[0, 8], z_peer(3 * s8))

    def d_sent():
        all_of(sr, ds_send.at[0], ds_recv.at[0]).wait_send()
        all_of(zr.at[pl.ds(0, 15)], d_send.at[0], ds_recv.at[0]).wait_send()

    def d_send_on(side, m, below=()):
        place = slot(side, m)
        total = chip(place)
        for n in below:
            if n == 8:
                d_copy8().wait_recv()
                total += zr[slot(0, 8)].astype(F32)
            else:
                d_copy(side, n).wait_recv()
                total += zr[slot(side, n)].astype(F32)
        zs[place] = total.astype(BF16)
        start(d_copy(side, m))

    a_sibling(2, OWN)
    for m in (1, 2):
        for side in (0, 1):
            start(a_copy(side, m, OWN))
    start(a_copy(1, 3, OWN))
    for side in (0, 1):
        start(a_copy(side, 5, OWN))
    for m in (1, 2):
        for side in (0, 1):
            a_take(side, m)
    start(a_copy(0, 3, slot(0, 2)))
    a_take(1, 3)
    load_in.wait()
    load_b_in.wait()
    load_b_out.wait()
    a_sibling_wait(2)
    assemble(2)
    project_in(2)
    b_start(2)
    for side in (0, 1):
        a_take(side, 5)
        for m in (4, 7, 6):
            start(a_copy(side, m, slot(side, 5)))
    start(a_copy8())
    a_take(0, 3)
    for side in (0, 1):
        a_take(side, 4)
    a_sibling_wait(0)
    assemble(0)
    project_in(0)
    b_start(0)
    for m in (6, 7):
        for side in (0, 1):
            a_take(side, m)
    a_copy8().wait_recv()
    a_sibling(1, slot(0, 8))
    a_sibling_wait(1)
    assemble(1)
    project_in(1)
    b_start(1)
    load_out.wait()
    a_sent()
    b_finish(2)
    b_finish(0)
    c_start(0)
    b_finish(1)
    c_start(1)
    c_wait(0)
    project_out(0)
    d_sibling_start(0)
    c_start(2)
    d_sibling(0).wait_recv()
    for side in (0, 1):
        d_send_on(side, 4)
    d_send_on(0, 3)
    c_wait(1)
    project_out(1)
    d_sibling_start(1)
    d_sibling(1).wait_recv()
    zs[slot(0, 8)] = chip(slot(0, 8)).astype(BF16)
    start(d_copy8())
    for m in (7, 6):
        for side in (0, 1):
            d_send_on(side, m)
    c_wait(2)
    project_out(2)
    d_sibling_start(2)
    for g in range(GROUPS):
        plane_sent(g)
    d_sibling(2).wait_recv()
    for m in (2, 1):
        for side in (0, 1):
            d_send_on(side, m)
    d_send_on(1, 3)
    d_send_on(1 - c, 5, (6, 7))
    d_send_on(c, 5, (6, 7, 8))
    total = chip(OWN)
    for m in (1, 2, 3, 4, 5):
        for side in (0, 1):
            d_copy(side, m).wait_recv()
            total += zr[slot(side, m)].astype(F32)
    last = jnp.where(c == 0, total[8:12], total[12:16])
    out = jnp.concatenate([total[0:8], last], axis=0) + b_out[...].reshape(1, -1)
    o_ref[...] = out.astype(BF16)
    d_sent()


def on_device(tokens, w_in, b_in, w_out, b_out):
    width, hidden = w_in.shape
    half = hidden // 2
    vmem = pl.BlockSpec(memory_space=pltpu.VMEM)
    hbm = pl.BlockSpec(memory_space=pltpu.HBM)
    dma = pltpu.SemaphoreType.DMA
    return pl.pallas_call(
        kernel,
        out_shape=jax.ShapeDtypeStruct(tokens.shape, BF16),
        in_specs=[hbm] * 5,
        out_specs=vmem,
        scratch_shapes=[
            pltpu.VMEM(tokens.shape, BF16),
            pltpu.VMEM((width, hidden), BF16),
            pltpu.VMEM(b_in.shape, F32),
            pltpu.VMEM((hidden, width), BF16),
            pltpu.VMEM(b_out.shape, F32),
            pltpu.VMEM((2, 16, 16, width), BF16),
            pltpu.VMEM((384, width), BF16),
            pltpu.VMEM((GROUPS, 8, 2, 16, half), F32),
            pltpu.VMEM((GROUPS, 8, 2, 16, half), BF16),
            pltpu.VMEM((GROUPS, 16, 16, half), BF16),
            pltpu.VMEM((GROUPS, 8, 2, 16, half), BF16),
            pltpu.VMEM((384, width), F32),
            pltpu.VMEM((16, 16, width), BF16),
            pltpu.VMEM((16, 16, width), BF16),
            pltpu.VMEM((16, 16, width), BF16),
            pltpu.VMEM((16, 16, width), BF16),
            dma((5,)),
            dma((1,)), dma((2, 9)),
            dma((1,)), dma((GROUPS,)),
            dma((GROUPS,)), dma((GROUPS,)),
            dma((GROUPS,)), dma((GROUPS,)),
            dma((1,)), dma((GROUPS,)),
            dma((1,)), dma((2, 9)),
        ],
        compiler_params=pltpu.CompilerParams(
            collective_id=0, has_side_effects=True, vmem_limit_bytes=60 * 2**20
        ),
        cost_estimate=pl.CostEstimate(
            flops=4 * 384 * width * hidden, bytes_accessed=4 * width * hidden, transcendentals=384 * hidden // 16
        ),
    )(tokens, w_in, b_in, w_out, b_out)


def solution(mesh):
    return jax.shard_map(
        on_device,
        mesh=mesh,
        in_specs=(P("row", "col"), P("col", "row"), P("row"), P("row", "col"), P("col")),
        out_specs=P("row", "col"),
        check_vma=False,
    )
```

```python
import functools

import jax
import jax.numpy as jnp
from jax import lax
from jax.experimental import pallas as pl
from jax.experimental.pallas import tpu as pltpu
from jax.sharding import PartitionSpec as P

BF16 = jnp.bfloat16
F32 = jnp.float32
PARENT = {1: 0, 2: 0, 5: 0, 3: 2, 4: 5, 6: 5, 7: 5, 8: 5}
PARENT_OUT = {1: 0, 2: 0, 3: 0, 4: 0, 5: 0, 6: 5, 7: 5, 8: 5}
SPLIT, OWN = 10, 11
PLANE = [(dy, dx) for dy in (2, 1, 3, 0) for dx in (2, 1, 3, 0) if (dy, dx) != (0, 0)]
GROUPS = 3
CHUNKS = ((0, 5), (5, 10), (11, 16))
PARTS = ((0, 5), (5, 10), (10, 16))


def slot(side, m):
    if m == 3:
        return (2, SPLIT)[side]
    return {5: 0, 4: 3, 8: 5, 7: 6, 6: 8, 1: 12, 2: 14}[m] + side


def pack(first, last):
    tiles = first.shape[1] // 128
    groups = [first[:, 128 * t : 128 * t + 128] for t in range(tiles)]
    ends = [last[:, 128 * t : 128 * t + 128] for t in range(tiles)]
    if tiles % 2:
        ends.append(jnp.zeros_like(ends[0]))
    groups += [jnp.concatenate(ends[t : t + 2], axis=0) for t in range(0, len(ends), 2)]
    if len(groups) % 2:
        groups.append(jnp.zeros_like(groups[0]))
    return jnp.concatenate(groups, axis=0)


def packed_rows(tiles):
    groups = tiles + (tiles + 1) // 2
    return 8 * (groups + groups % 2)


def first_of(packed, t):
    return packed[8 * t : 8 * t + 8]


def last_of(packed, t, tiles):
    at = 8 * (tiles + t // 2) + 4 * (t % 2)
    return packed[at : at + 4]


def first_row(place):
    if not isinstance(place, int):
        return 24 * place
    group = 0 if place < 5 else 1 if place < 10 else 2
    return 128 * group + 24 * (place - CHUNKS[group][0])


def kernel(
    tok_hbm, win_ref, bin_hbm, wout_ref, bout_hbm, o_ref,
    tok, win, b_in, wout, b_out, ta, xs, pf, pb, rb, hid, po, ss, sr, zs, zr,
    wsem, a_send, a_recv, as_send, as_recv, b_send, b_recv, c_send, c_recv,
    ds_send, ds_recv, d_send, d_recv,
):
    row, col = lax.axis_index("row"), lax.axis_index("col")
    z, c = row // 2, row % 2
    y, x = col // 4, col % 4
    half = pb.shape[-1]
    tiles = xs.shape[1] // 128
    s8 = 1 - 2 * c

    def z_peer(dz):
        return {"row": lax.rem(z + dz + 16, 16) * 2 + c, "col": col}

    def plane_col(dy, dx):
        return lax.rem(y + dy + 4, 4) * 4 + lax.rem(x + dx + 4, 4)

    def plane_peer(dy, dx):
        return {"row": row, "col": plane_col(dy, dx)}

    sibling = {"row": z * 2 + (1 - c), "col": col}

    def remote(src, dst, send, recv, peer):
        return pltpu.make_async_remote_copy(
            src_ref=src, dst_ref=dst, send_sem=send, recv_sem=recv,
            device_id=peer, device_id_type=pl.DeviceIdType.MESH,
        )

    def start(copy):
        copy.start()

    def all_of(block, send, recv):
        return remote(block, block, send, recv, sibling)

    load_tok = pltpu.make_async_copy(tok_hbm, tok, wsem.at[2])
    load_tok.start()

    barrier = pltpu.get_barrier_semaphore()
    peers = [z_peer(dz) for dz in (5, -5, 4, -4, 3, -3, 2, -2, 1, -1)]
    peers += [plane_peer(dy, dx) for dy, dx in PLANE] + [sibling]
    for peer in peers:
        pl.semaphore_signal(barrier, inc=1, device_id=peer, device_id_type=pl.DeviceIdType.MESH)
    load_in = pltpu.make_async_copy(win_ref, win, wsem.at[0])
    load_out = pltpu.make_async_copy(wout_ref, wout, wsem.at[1])
    load_b_in = pltpu.make_async_copy(bin_hbm, b_in, wsem.at[3])
    load_b_out = pltpu.make_async_copy(bout_hbm, b_out, wsem.at[4])
    for load in (load_in, load_out, load_b_in, load_b_out):
        load.start()
    load_tok.wait()

    own = tok[...].astype(F32)
    ta[c, OWN] = pack(own[0:8], own[8:12]).astype(BF16)
    pl.semaphore_wait(barrier, len(peers))

    def a_copy(side, m, at):
        sign = 1 - 2 * side
        dz = -sign * (m - (0 if m == 3 and side == 1 else PARENT[m]))
        place = slot(side, m)
        return remote(ta.at[c, at], ta.at[c, place], a_send.at[0], a_recv.at[side, m], z_peer(dz))

    def a_copy8():
        return remote(ta.at[c, slot(0, 5) + c], ta.at[c, slot(0, 8)], a_send.at[0], a_recv.at[0, 8], z_peer(-3 * s8))

    def a_wait(side, m):
        a_copy(side, m, 0).wait_recv()

    def a_sibling(g, place):
        start(remote(ta.at[c, place], ta.at[c, place], as_send.at[0], as_recv.at[g], sibling))

    def a_sibling_wait(g):
        part = pl.ds(PARTS[g][0], PARTS[g][1] - PARTS[g][0])
        all_of(ta.at[1 - c, part], as_send.at[0], as_recv.at[g]).wait_recv()

    def a_take(side, m):
        a_wait(side, m)
        place = slot(side, m)
        a_sibling(0 if place < 5 else 1 if place < 10 else 2, place)

    def a_sent():
        all_of(ta.at[c, pl.ds(0, 15)], a_send.at[0], as_recv.at[0]).wait_send()
        all_of(ta.at[c], as_send.at[0], as_recv.at[0]).wait_send()

    def assemble(g):
        chunks = [(ta[0, k].astype(F32), ta[1, k].astype(F32)) for k in (*range(*CHUNKS[g]), SPLIT)]
        for t in range(tiles):
            rows = []
            for first, second in chunks:
                rows += [first_of(first, t), first_of(second, t)]
                rows += [last_of(first, t, tiles), last_of(second, t, tiles)]
            rows[-4:] = (rows[-4:-3], rows[-3:-2], rows[-2:])[g]
            xs[128 * g : 128 * g + 128, 128 * t : 128 * t + 128] = jnp.concatenate(rows, axis=0).astype(BF16)

    def project_in(g):
        lhs = xs[128 * g : 128 * g + 128, :]

        @pl.loop(0, 2)
        def _(h):
            cols = pl.ds(pl.multiple_of(h * half, 128), half)
            part = jnp.dot(lhs, win[:, cols], preferred_element_type=F32).reshape(8, 16, half)
            pf[g, :, h] = part
            pb[g, :, h] = part.astype(BF16)

    def b_copy(g, dy, dx):
        there = plane_col(dy, dx)
        d = dy * 4 + dx
        return remote(
            pb.at[g, there // 2, there % 2], rb.at[g, d], b_send.at[g], b_recv.at[g], plane_peer(dy, dx)
        )

    def b_start(g):
        for dy, dx in PLANE:
            start(b_copy(g, dy, dx))

    def b_finish(g):
        total = pf[g, col // 2, col % 2]
        blocks = all_of(rb.at[g, pl.ds(1, 15)], b_send.at[g], b_recv.at[g])
        blocks.wait_recv()
        for dy, dx in PLANE:
            total += rb[g, dy * 4 + dx].astype(F32)
        v = total + b_in[pl.ds(pl.multiple_of((col % 2) * half, 128), half)].reshape(1, half)
        v = 0.5 * v * (1.0 + jnp.tanh(0.7978845608 * (v + 0.044715 * (v * v * v))))
        hid[g, col // 2, col % 2] = v.astype(BF16)

    def c_start(g):
        block = hid.at[g, col // 2, col % 2]
        for dy, dx in PLANE:
            start(remote(block, block, c_send.at[g], c_recv.at[g], plane_peer(dy, dx)))

    def c_wait(g):
        all_of(rb.at[g, pl.ds(1, 15)], c_send.at[g], c_recv.at[g]).wait_recv()

    def plane_sent(g):
        all_of(rb.at[g, pl.ds(1, 15)], b_send.at[g], b_recv.at[g]).wait_send()
        all_of(rb.at[g, pl.ds(1, 15)], c_send.at[g], c_recv.at[g]).wait_send()

    def project_out(g):
        total = jnp.zeros((128, po.shape[1]), F32)
        for h in range(2):
            lhs = hid[g, :, h].reshape(128, half)
            total += jnp.dot(lhs, wout[h * half : (h + 1) * half, :], preferred_element_type=F32)
        po[128 * g : 128 * g + 128, :] = total

    def share(k, core):
        if isinstance(k, int) and k == SPLIT:
            first, rest = 128 * core + 120, 256 + 120
        else:
            first, rest = first_row(k) + 8 * core, first_row(k) + 16
        first, rest = (po[pl.ds(pl.multiple_of(at, 8), 8), :] for at in (first, rest))
        return pack(first, jnp.where(core == 0, rest[0:4], rest[4:8]))

    def d_sibling_one(k):
        return remote(ss.at[k], sr.at[k], ds_send.at[0], ds_recv.at[k], sibling)

    def d_sibling_start_one(k):
        ss[k] = share(k, 1 - c).astype(BF16)
        start(d_sibling_one(k))

    def d_sibling(g):
        part = pl.ds(CHUNKS[g][0], 5)
        return remote(ss.at[part], sr.at[part], ds_send.at[0], ds_recv.at[CHUNKS[g][0]], sibling)

    def d_sibling_start(g):
        for k in range(*CHUNKS[g]):
            ss[k] = share(k, 1 - c).astype(BF16)
        start(d_sibling(g))

    def chip(k):
        return share(k, c) + sr[k].astype(F32)

    def d_copy(side, m):
        dz = (1 - 2 * side) * (m - PARENT_OUT[m])
        place = slot(side, m)
        return remote(zs.at[place], zr.at[place], d_send.at[0], d_recv.at[side, m], z_peer(dz))

    def d_copy8():
        return remote(zs.at[slot(0, 8)], zr.at[slot(0, 8)], d_send.at[0], d_recv.at[0, 8], z_peer(3 * s8))

    def d_sent():
        all_of(sr, ds_send.at[0], ds_recv.at[0]).wait_send()
        all_of(zr.at[pl.ds(0, 15)], d_send.at[0], ds_recv.at[0]).wait_send()

    def d_send_on(side, m, below=()):
        place = slot(side, m)
        total = chip(place)
        for n in below:
            if n == 8:
                d_copy8().wait_recv()
                total += zr[slot(0, 8)].astype(F32)
            else:
                d_copy(side, n).wait_recv()
                total += zr[slot(side, n)].astype(F32)
        zs[place] = total.astype(BF16)
        start(d_copy(side, m))

    for m in (5, 1, 2):
        for side in (0, 1):
            start(a_copy(side, m, OWN))
    start(a_copy(1, 3, OWN))
    a_sibling(2, OWN)
    for m in (1, 2):
        for side in (0, 1):
            a_take(side, m)
    start(a_copy(0, 3, slot(0, 2)))
    for side in (0, 1):
        a_wait(side, 5)
        start(a_copy(side, 4, slot(side, 5)))
    start(a_copy8())
    for m in (7, 6):
        for side in (0, 1):
            start(a_copy(side, m, slot(side, 5)))
    a_take(1, 3)
    for side in (0, 1):
        a_sibling(0, slot(side, 5))
    load_in.wait()
    load_b_in.wait()
    load_b_out.wait()
    a_sibling_wait(2)
    assemble(2)
    project_in(2)
    b_start(2)
    a_take(0, 3)
    for side in (0, 1):
        a_take(side, 4)
    a_sibling_wait(0)
    assemble(0)
    project_in(0)
    b_start(0)
    for m in (6, 7):
        for side in (0, 1):
            a_take(side, m)
    a_copy8().wait_recv()
    a_sibling(1, slot(0, 8))
    a_sibling_wait(1)
    assemble(1)
    project_in(1)
    b_start(1)
    load_out.wait()
    a_sent()
    b_finish(2)
    b_finish(0)
    c_start(0)
    b_finish(1)
    c_start(1)
    c_wait(0)
    project_out(0)
    d_sibling_start(0)
    c_start(2)
    d_sibling(0).wait_recv()
    for side in (0, 1):
        d_send_on(side, 4)
    d_send_on(0, 3)
    c_wait(1)
    project_out(1)
    for k in (slot(0, 8), slot(0, 7), slot(1, 7), slot(0, 6), slot(1, 6)):
        d_sibling_start_one(k)
    d_sibling_one(slot(0, 8)).wait_recv()
    zs[slot(0, 8)] = chip(slot(0, 8)).astype(BF16)
    start(d_copy8())
    for m in (7, 6):
        for side in (0, 1):
            d_sibling_one(slot(side, m)).wait_recv()
            d_send_on(side, m)
    c_wait(2)
    project_out(2)
    d_sibling_start_one(SPLIT)
    d_sibling_start(2)
    d_send_on(1 - c, 5, (6, 7))
    d_send_on(c, 5, (6, 7, 8))
    d_sibling_one(SPLIT).wait_recv()
    d_send_on(1, 3)
    d_sibling(2).wait_recv()
    for m in (2, 1):
        for side in (0, 1):
            d_send_on(side, m)
    for g in range(GROUPS):
        plane_sent(g)
    total = chip(OWN)
    for m in (1, 2, 3, 4, 5):
        for side in (0, 1):
            d_copy(side, m).wait_recv()
            total += zr[slot(side, m)].astype(F32)
    first = jnp.concatenate([first_of(total, t) for t in range(tiles)], axis=1)
    last = jnp.concatenate([last_of(total, t, tiles) for t in range(tiles)], axis=1)
    out = jnp.concatenate([first, last], axis=0) + b_out[...].reshape(1, -1)
    o_ref[...] = out.astype(BF16)
    d_sent()


def on_device(tokens, w_in, b_in, w_out, b_out):
    width, hidden = w_in.shape
    half = hidden // 2
    chunk = packed_rows(width // 128)
    vmem = pl.BlockSpec(memory_space=pltpu.VMEM)
    hbm = pl.BlockSpec(memory_space=pltpu.HBM)
    dma = pltpu.SemaphoreType.DMA
    return pl.pallas_call(
        kernel,
        out_shape=jax.ShapeDtypeStruct(tokens.shape, BF16),
        in_specs=[hbm] * 5,
        out_specs=vmem,
        scratch_shapes=[
            pltpu.VMEM(tokens.shape, BF16),
            pltpu.VMEM((width, hidden), BF16),
            pltpu.VMEM(b_in.shape, F32),
            pltpu.VMEM((hidden, width), BF16),
            pltpu.VMEM(b_out.shape, F32),
            pltpu.VMEM((2, 16, chunk, 128), BF16),
            pltpu.VMEM((384, width), BF16),
            pltpu.VMEM((GROUPS, 8, 2, 16, half), F32),
            pltpu.VMEM((GROUPS, 8, 2, 16, half), BF16),
            pltpu.VMEM((GROUPS, 16, 16, half), BF16),
            pltpu.VMEM((GROUPS, 8, 2, 16, half), BF16),
            pltpu.VMEM((384, width), F32),
            pltpu.VMEM((16, chunk, 128), BF16),
            pltpu.VMEM((16, chunk, 128), BF16),
            pltpu.VMEM((16, chunk, 128), BF16),
            pltpu.VMEM((16, chunk, 128), BF16),
            dma((5,)),
            dma((1,)), dma((2, 9)),
            dma((1,)), dma((GROUPS,)),
            dma((GROUPS,)), dma((GROUPS,)),
            dma((GROUPS,)), dma((GROUPS,)),
            dma((1,)), dma((16,)),
            dma((1,)), dma((2, 9)),
        ],
        compiler_params=pltpu.CompilerParams(
            collective_id=0, has_side_effects=True, vmem_limit_bytes=60 * 2**20
        ),
        cost_estimate=pl.CostEstimate(
            flops=4 * 384 * width * hidden, bytes_accessed=4 * width * hidden, transcendentals=384 * hidden // 16
        ),
    )(tokens, w_in, b_in, w_out, b_out)


def solution(mesh):
    return jax.shard_map(
        on_device,
        mesh=mesh,
        in_specs=(P("row", "col"), P("col", "row"), P("row"), P("row", "col"), P("col")),
        out_specs=P("row", "col"),
        check_vma=False,
    )
```

```python
import functools

import jax
import jax.numpy as jnp
from jax import lax
from jax.experimental import pallas as pl
from jax.experimental.pallas import tpu as pltpu
from jax.sharding import PartitionSpec as P

BF16 = jnp.bfloat16
F32 = jnp.float32
PARENT = {1: 0, 2: 0, 5: 0, 3: 2, 4: 5, 6: 5, 7: 5, 8: 5}
PARENT_OUT = {1: 0, 2: 0, 3: 0, 4: 0, 5: 4, 6: 4, 7: 4, 8: 4}
SPLIT, OWN = 10, 11
PLANE = [(dy, dx) for dy in (2, 1, 3, 0) for dx in (2, 1, 3, 0) if (dy, dx) != (0, 0)]
GROUPS = 3
CHUNKS = ((0, 5), (5, 10), (11, 16))
PARTS = ((0, 5), (5, 10), (10, 16))


def slot(side, m):
    if m == 3:
        return (2, SPLIT)[side]
    return {5: 0, 4: 3, 8: 5, 7: 6, 6: 8, 1: 12, 2: 14}[m] + side


def pack(first, last):
    tiles = first.shape[1] // 128
    groups = [first[:, 128 * t : 128 * t + 128] for t in range(tiles)]
    ends = [last[:, 128 * t : 128 * t + 128] for t in range(tiles)]
    if tiles % 2:
        ends.append(jnp.zeros_like(ends[0]))
    groups += [jnp.concatenate(ends[t : t + 2], axis=0) for t in range(0, len(ends), 2)]
    if len(groups) % 2:
        groups.append(jnp.zeros_like(groups[0]))
    return jnp.concatenate(groups, axis=0)


def packed_rows(tiles):
    groups = tiles + (tiles + 1) // 2
    return 8 * (groups + groups % 2)


def first_of(packed, t):
    return packed[8 * t : 8 * t + 8]


def last_of(packed, t, tiles):
    at = 8 * (tiles + t // 2) + 4 * (t % 2)
    return packed[at : at + 4]


def first_row(place):
    if not isinstance(place, int):
        return 24 * place
    group = 0 if place < 5 else 1 if place < 10 else 2
    return 128 * group + 24 * (place - CHUNKS[group][0])


def kernel(
    tok_hbm, win_ref, bin_hbm, wout_ref, bout_hbm, o_ref,
    tok, win, b_in, wout, b_out, ta, xs, pf, pb, rb, hid, po, ss, sr, zs, zr,
    wsem, a_send, a_recv, as_send, as_recv, b_send, b_recv, c_send, c_recv,
    ds_send, ds_recv, d_send, d_recv,
):
    row, col = lax.axis_index("row"), lax.axis_index("col")
    z, c = row // 2, row % 2
    y, x = col // 4, col % 4
    half = pb.shape[-1]
    tiles = xs.shape[1] // 128
    s8 = 1 - 2 * c

    def z_peer(dz):
        return {"row": lax.rem(z + dz + 16, 16) * 2 + c, "col": col}

    def plane_col(dy, dx):
        return lax.rem(y + dy + 4, 4) * 4 + lax.rem(x + dx + 4, 4)

    def plane_peer(dy, dx):
        return {"row": row, "col": plane_col(dy, dx)}

    sibling = {"row": z * 2 + (1 - c), "col": col}

    def remote(src, dst, send, recv, peer):
        return pltpu.make_async_remote_copy(
            src_ref=src, dst_ref=dst, send_sem=send, recv_sem=recv,
            device_id=peer, device_id_type=pl.DeviceIdType.MESH,
        )

    def start(copy):
        copy.start()

    def all_of(block, send, recv):
        return remote(block, block, send, recv, sibling)

    load_tok = pltpu.make_async_copy(tok_hbm, tok, wsem.at[2])
    load_tok.start()

    barrier = pltpu.get_barrier_semaphore()
    peers = [z_peer(dz) for dz in (5, -5, 4, -4, 3, -3, 2, -2, 1, -1)]
    peers += [plane_peer(dy, dx) for dy, dx in PLANE] + [sibling]
    for peer in peers:
        pl.semaphore_signal(barrier, inc=1, device_id=peer, device_id_type=pl.DeviceIdType.MESH)
    load_in = pltpu.make_async_copy(win_ref, win, wsem.at[0])
    load_out = pltpu.make_async_copy(wout_ref, wout, wsem.at[1])
    load_b_in = pltpu.make_async_copy(bin_hbm, b_in, wsem.at[3])
    load_b_out = pltpu.make_async_copy(bout_hbm, b_out, wsem.at[4])
    for load in (load_in, load_out, load_b_in, load_b_out):
        load.start()
    load_tok.wait()

    own = tok[...].astype(F32)
    ta[c, OWN] = pack(own[0:8], own[8:12]).astype(BF16)
    pl.semaphore_wait(barrier, len(peers))

    def a_copy(side, m, at):
        sign = 1 - 2 * side
        dz = -sign * (m - (0 if m == 3 and side == 1 else PARENT[m]))
        place = slot(side, m)
        return remote(ta.at[c, at], ta.at[c, place], a_send.at[0], a_recv.at[side, m], z_peer(dz))

    def a_copy8():
        return remote(ta.at[c, slot(0, 5) + c], ta.at[c, slot(0, 8)], a_send.at[0], a_recv.at[0, 8], z_peer(-3 * s8))

    def a_wait(side, m):
        a_copy(side, m, 0).wait_recv()

    def a_sibling(g, place):
        start(remote(ta.at[c, place], ta.at[c, place], as_send.at[0], as_recv.at[g], sibling))

    def a_sibling_wait(g):
        part = pl.ds(PARTS[g][0], PARTS[g][1] - PARTS[g][0])
        all_of(ta.at[1 - c, part], as_send.at[0], as_recv.at[g]).wait_recv()

    def a_take(side, m):
        a_wait(side, m)
        place = slot(side, m)
        a_sibling(0 if place < 5 else 1 if place < 10 else 2, place)

    def a_sent():
        all_of(ta.at[c, pl.ds(0, 15)], a_send.at[0], as_recv.at[0]).wait_send()
        all_of(ta.at[c], as_send.at[0], as_recv.at[0]).wait_send()

    def assemble(g):
        chunks = [(ta[0, k].astype(F32), ta[1, k].astype(F32)) for k in (*range(*CHUNKS[g]), SPLIT)]
        for t in range(tiles):
            rows = []
            for first, second in chunks:
                rows += [first_of(first, t), first_of(second, t)]
                rows += [last_of(first, t, tiles), last_of(second, t, tiles)]
            rows[-4:] = (rows[-4:-3], rows[-3:-2], rows[-2:])[g]
            xs[128 * g : 128 * g + 128, 128 * t : 128 * t + 128] = jnp.concatenate(rows, axis=0).astype(BF16)

    def project_in(g):
        lhs = xs[128 * g : 128 * g + 128, :]

        @pl.loop(0, 2)
        def _(h):
            cols = pl.ds(pl.multiple_of(h * half, 128), half)
            part = jnp.dot(lhs, win[:, cols], preferred_element_type=F32).reshape(8, 16, half)
            pf[g, :, h] = part
            pb[g, :, h] = part.astype(BF16)

    def b_copy(g, dy, dx):
        there = plane_col(dy, dx)
        d = dy * 4 + dx
        return remote(
            pb.at[g, there // 2, there % 2], rb.at[g, d], b_send.at[g], b_recv.at[g], plane_peer(dy, dx)
        )

    def b_start(g):
        for dy, dx in PLANE:
            start(b_copy(g, dy, dx))

    def b_finish(g):
        total = pf[g, col // 2, col % 2]
        blocks = all_of(rb.at[g, pl.ds(1, 15)], b_send.at[g], b_recv.at[g])
        blocks.wait_recv()
        for dy, dx in PLANE:
            total += rb[g, dy * 4 + dx].astype(F32)
        v = total + b_in[pl.ds(pl.multiple_of((col % 2) * half, 128), half)].reshape(1, half)
        v = 0.5 * v * (1.0 + jnp.tanh(0.7978845608 * (v + 0.044715 * (v * v * v))))
        hid[g, col // 2, col % 2] = v.astype(BF16)

    def c_start(g):
        block = hid.at[g, col // 2, col % 2]
        for dy, dx in PLANE:
            start(remote(block, block, c_send.at[g], c_recv.at[g], plane_peer(dy, dx)))

    def c_wait(g):
        all_of(rb.at[g, pl.ds(1, 15)], c_send.at[g], c_recv.at[g]).wait_recv()

    def plane_sent(g):
        all_of(rb.at[g, pl.ds(1, 15)], b_send.at[g], b_recv.at[g]).wait_send()
        all_of(rb.at[g, pl.ds(1, 15)], c_send.at[g], c_recv.at[g]).wait_send()

    def project_out(g):
        total = jnp.zeros((128, po.shape[1]), F32)
        for h in range(2):
            lhs = hid[g, :, h].reshape(128, half)
            total += jnp.dot(lhs, wout[h * half : (h + 1) * half, :], preferred_element_type=F32)
        po[128 * g : 128 * g + 128, :] = total

    def share(k, core):
        if isinstance(k, int) and k == SPLIT:
            first, rest = 128 * core + 120, 256 + 120
        else:
            first, rest = first_row(k) + 8 * core, first_row(k) + 16
        first, rest = (po[pl.ds(pl.multiple_of(at, 8), 8), :] for at in (first, rest))
        return pack(first, jnp.where(core == 0, rest[0:4], rest[4:8]))

    def d_sibling_one(k):
        return remote(ss.at[k], sr.at[k], ds_send.at[0], ds_recv.at[k], sibling)

    def d_sibling_start_one(k):
        ss[k] = share(k, 1 - c).astype(BF16)
        start(d_sibling_one(k))

    def d_sibling(g):
        part = pl.ds(CHUNKS[g][0], 5)
        return remote(ss.at[part], sr.at[part], ds_send.at[0], ds_recv.at[CHUNKS[g][0]], sibling)

    def d_sibling_start(g):
        for k in range(*CHUNKS[g]):
            ss[k] = share(k, 1 - c).astype(BF16)
        start(d_sibling(g))

    def chip(k):
        return share(k, c) + sr[k].astype(F32)

    def d_copy(side, m):
        dz = (1 - 2 * side) * (m - PARENT_OUT[m])
        place = slot(side, m)
        return remote(zs.at[place], zr.at[place], d_send.at[0], d_recv.at[side, m], z_peer(dz))

    def d_copy8():
        return remote(zs.at[slot(0, 8)], zr.at[slot(0, 8)], d_send.at[0], d_recv.at[0, 8], z_peer(4 * s8))

    def d_sent():
        all_of(sr, ds_send.at[0], ds_recv.at[0]).wait_send()
        all_of(zr.at[pl.ds(0, 15)], d_send.at[0], ds_recv.at[0]).wait_send()

    def d_send_on(side, m, below=()):
        place = slot(side, m)
        total = chip(place)
        for n in below:
            if n == 8:
                d_copy8().wait_recv()
                total += zr[slot(0, 8)].astype(F32)
            else:
                d_copy(side, n).wait_recv()
                total += zr[slot(side, n)].astype(F32)
        zs[place] = total.astype(BF16)
        start(d_copy(side, m))

    for m in (5, 1, 2):
        for side in (0, 1):
            start(a_copy(side, m, OWN))
    start(a_copy(1, 3, OWN))
    a_sibling(2, OWN)
    for m in (1, 2):
        for side in (0, 1):
            a_take(side, m)
    start(a_copy(0, 3, slot(0, 2)))
    for side in (0, 1):
        a_wait(side, 5)
    start(a_copy8())
    for m in (7, 6, 4):
        for side in (0, 1):
            start(a_copy(side, m, slot(side, 5)))
    a_take(1, 3)
    for side in (0, 1):
        a_sibling(0, slot(side, 5))
    load_in.wait()
    load_b_in.wait()
    load_b_out.wait()
    a_sibling_wait(2)
    assemble(2)
    project_in(2)
    b_start(2)
    for m in (6, 7):
        for side in (0, 1):
            a_take(side, m)
    a_copy8().wait_recv()
    a_sibling(1, slot(0, 8))
    a_take(0, 3)
    for side in (0, 1):
        a_take(side, 4)
    a_sibling_wait(1)
    assemble(1)
    project_in(1)
    b_start(1)
    a_sibling_wait(0)
    assemble(0)
    project_in(0)
    b_start(0)
    load_out.wait()
    a_sent()
    b_finish(2)
    b_finish(1)
    c_start(1)
    b_finish(0)
    c_start(0)
    c_wait(1)
    project_out(1)
    for k in (slot(0, 8), slot(0, 7), slot(1, 7), slot(0, 6), slot(1, 6)):
        d_sibling_start_one(k)
    c_start(2)
    d_sibling_one(slot(0, 8)).wait_recv()
    zs[slot(0, 8)] = chip(slot(0, 8)).astype(BF16)
    start(d_copy8())
    for m in (7, 6):
        for side in (0, 1):
            d_sibling_one(slot(side, m)).wait_recv()
            d_send_on(side, m)
    c_wait(0)
    project_out(0)
    d_sibling_start(0)
    d_sibling(0).wait_recv()
    for side in (0, 1):
        d_send_on(side, 5)
    d_send_on(0, 3)
    c_wait(2)
    project_out(2)
    d_sibling_start_one(SPLIT)
    d_sibling_start(2)
    d_send_on(1 - c, 4, (5, 6, 7))
    d_send_on(c, 4, (5, 6, 7, 8))
    d_sibling_one(SPLIT).wait_recv()
    d_send_on(1, 3)
    d_sibling(2).wait_recv()
    for m in (2, 1):
        for side in (0, 1):
            d_send_on(side, m)
    for g in range(GROUPS):
        plane_sent(g)
    total = chip(OWN)
    for m in (1, 2, 3, 4):
        for side in (0, 1):
            d_copy(side, m).wait_recv()
            total += zr[slot(side, m)].astype(F32)
    first = jnp.concatenate([first_of(total, t) for t in range(tiles)], axis=1)
    last = jnp.concatenate([last_of(total, t, tiles) for t in range(tiles)], axis=1)
    out = jnp.concatenate([first, last], axis=0) + b_out[...].reshape(1, -1)
    o_ref[...] = out.astype(BF16)
    d_sent()


def on_device(tokens, w_in, b_in, w_out, b_out):
    width, hidden = w_in.shape
    half = hidden // 2
    chunk = packed_rows(width // 128)
    vmem = pl.BlockSpec(memory_space=pltpu.VMEM)
    hbm = pl.BlockSpec(memory_space=pltpu.HBM)
    dma = pltpu.SemaphoreType.DMA
    return pl.pallas_call(
        kernel,
        out_shape=jax.ShapeDtypeStruct(tokens.shape, BF16),
        in_specs=[hbm] * 5,
        out_specs=vmem,
        scratch_shapes=[
            pltpu.VMEM(tokens.shape, BF16),
            pltpu.VMEM((width, hidden), BF16),
            pltpu.VMEM(b_in.shape, F32),
            pltpu.VMEM((hidden, width), BF16),
            pltpu.VMEM(b_out.shape, F32),
            pltpu.VMEM((2, 16, chunk, 128), BF16),
            pltpu.VMEM((384, width), BF16),
            pltpu.VMEM((GROUPS, 8, 2, 16, half), F32),
            pltpu.VMEM((GROUPS, 8, 2, 16, half), BF16),
            pltpu.VMEM((GROUPS, 16, 16, half), BF16),
            pltpu.VMEM((GROUPS, 8, 2, 16, half), BF16),
            pltpu.VMEM((384, width), F32),
            pltpu.VMEM((16, chunk, 128), BF16),
            pltpu.VMEM((16, chunk, 128), BF16),
            pltpu.VMEM((16, chunk, 128), BF16),
            pltpu.VMEM((16, chunk, 128), BF16),
            dma((5,)),
            dma((1,)), dma((2, 9)),
            dma((1,)), dma((GROUPS,)),
            dma((GROUPS,)), dma((GROUPS,)),
            dma((GROUPS,)), dma((GROUPS,)),
            dma((1,)), dma((16,)),
            dma((1,)), dma((2, 9)),
        ],
        compiler_params=pltpu.CompilerParams(
            collective_id=0, has_side_effects=True, vmem_limit_bytes=60 * 2**20
        ),
        cost_estimate=pl.CostEstimate(
            flops=4 * 384 * width * hidden, bytes_accessed=4 * width * hidden, transcendentals=384 * hidden // 16
        ),
    )(tokens, w_in, b_in, w_out, b_out)


def solution(mesh):
    return jax.shard_map(
        on_device,
        mesh=mesh,
        in_specs=(P("row", "col"), P("col", "row"), P("row"), P("row", "col"), P("col")),
        out_specs=P("row", "col"),
        check_vma=False,
    )
```

```python
import functools

import jax
import jax.numpy as jnp
from jax import lax
from jax.experimental import pallas as pl
from jax.experimental.pallas import tpu as pltpu
from jax.sharding import PartitionSpec as P

BF16 = jnp.bfloat16
F32 = jnp.float32
PARENT = {1: 0, 2: 0, 5: 0, 3: 2, 4: 5, 6: 5, 7: 5, 8: 5}
PARENT_OUT = {1: 0, 2: 0, 3: 0, 4: 0, 5: 4, 6: 4, 7: 4, 8: 4}
SPLIT, OWN = 10, 11
PLANE = [(dy, dx) for dy in (2, 1, 3, 0) for dx in (2, 1, 3, 0) if (dy, dx) != (0, 0)]
GROUPS = 3
CHUNKS = ((0, 5), (5, 10), (11, 16))
PARTS = ((0, 5), (5, 10), (10, 16))


def slot(side, m):
    if m == 3:
        return (2, SPLIT)[side]
    return {5: 0, 4: 3, 8: 5, 7: 6, 6: 8, 1: 12, 2: 14}[m] + side


def pack(first, last):
    tiles = first.shape[1] // 128
    groups = [first[:, 128 * t : 128 * t + 128] for t in range(tiles)]
    ends = [last[:, 128 * t : 128 * t + 128] for t in range(tiles)]
    if tiles % 2:
        ends.append(jnp.zeros_like(ends[0]))
    groups += [jnp.concatenate(ends[t : t + 2], axis=0) for t in range(0, len(ends), 2)]
    if len(groups) % 2:
        groups.append(jnp.zeros_like(groups[0]))
    return jnp.concatenate(groups, axis=0)


def packed_rows(tiles):
    groups = tiles + (tiles + 1) // 2
    return 8 * (groups + groups % 2)


def first_of(packed, t):
    return packed[8 * t : 8 * t + 8]


def last_of(packed, t, tiles):
    at = 8 * (tiles + t // 2) + 4 * (t % 2)
    return packed[at : at + 4]


def first_row(place):
    if not isinstance(place, int):
        return 24 * place
    group = 0 if place < 5 else 1 if place < 10 else 2
    return 128 * group + 24 * (place - CHUNKS[group][0])


def kernel(
    tok_hbm, win_ref, bin_hbm, wout_ref, bout_hbm, o_ref,
    tok, win, b_in, wout, b_out, ta, xs, pf, pb, rb, hid, po, ss, sr, zs, zr,
    wsem, a_send, a_recv, as_send, as_recv, b_send, b_recv, c_send, c_recv,
    ds_send, ds_recv, d_send, d_recv,
):
    row, col = lax.axis_index("row"), lax.axis_index("col")
    z, c = row // 2, row % 2
    y, x = col // 4, col % 4
    half = pb.shape[-1]
    tiles = xs.shape[1] // 128
    s8 = 1 - 2 * c

    def z_peer(dz):
        return {"row": lax.rem(z + dz + 16, 16) * 2 + c, "col": col}

    def plane_col(dy, dx):
        return lax.rem(y + dy + 4, 4) * 4 + lax.rem(x + dx + 4, 4)

    def plane_peer(dy, dx):
        return {"row": row, "col": plane_col(dy, dx)}

    sibling = {"row": z * 2 + (1 - c), "col": col}

    def remote(src, dst, send, recv, peer):
        return pltpu.make_async_remote_copy(
            src_ref=src, dst_ref=dst, send_sem=send, recv_sem=recv,
            device_id=peer, device_id_type=pl.DeviceIdType.MESH,
        )

    def start(copy):
        copy.start()

    def all_of(block, send, recv):
        return remote(block, block, send, recv, sibling)

    load_tok = pltpu.make_async_copy(tok_hbm, tok, wsem.at[2])
    load_tok.start()

    barrier = pltpu.get_barrier_semaphore()
    peers = [z_peer(dz) for dz in (5, -5, 4, -4, 3, -3, 2, -2, 1, -1)]
    peers += [plane_peer(dy, dx) for dy, dx in PLANE] + [sibling]
    for peer in peers:
        pl.semaphore_signal(barrier, inc=1, device_id=peer, device_id_type=pl.DeviceIdType.MESH)
    load_in = pltpu.make_async_copy(win_ref, win, wsem.at[0])
    load_out = pltpu.make_async_copy(wout_ref, wout, wsem.at[1])
    load_b_in = pltpu.make_async_copy(bin_hbm, b_in, wsem.at[3])
    load_b_out = pltpu.make_async_copy(bout_hbm, b_out, wsem.at[4])
    for load in (load_in, load_out, load_b_in, load_b_out):
        load.start()
    load_tok.wait()

    own = tok[...].astype(F32)
    ta[c, OWN] = pack(own[0:8], own[8:12]).astype(BF16)
    pl.semaphore_wait(barrier, len(peers))

    def a_copy(side, m, at):
        sign = 1 - 2 * side
        dz = -sign * (m - (0 if m == 3 and side == 1 else PARENT[m]))
        place = slot(side, m)
        return remote(ta.at[c, at], ta.at[c, place], a_send.at[0], a_recv.at[side, m], z_peer(dz))

    def a_copy8():
        return remote(ta.at[c, slot(0, 5) + c], ta.at[c, slot(0, 8)], a_send.at[0], a_recv.at[0, 8], z_peer(-3 * s8))

    def a_wait(side, m):
        a_copy(side, m, 0).wait_recv()

    def a_sibling(g, place):
        start(remote(ta.at[c, place], ta.at[c, place], as_send.at[0], as_recv.at[g], sibling))

    def a_sibling_wait(g):
        part = pl.ds(PARTS[g][0], PARTS[g][1] - PARTS[g][0])
        all_of(ta.at[1 - c, part], as_send.at[0], as_recv.at[g]).wait_recv()

    def a_take(side, m):
        a_wait(side, m)
        place = slot(side, m)
        a_sibling(0 if place < 5 else 1 if place < 10 else 2, place)

    def a_sent():
        all_of(ta.at[c, pl.ds(0, 15)], a_send.at[0], as_recv.at[0]).wait_send()
        all_of(ta.at[c], as_send.at[0], as_recv.at[0]).wait_send()

    def assemble(g):
        chunks = [(ta[0, k].astype(F32), ta[1, k].astype(F32)) for k in (*range(*CHUNKS[g]), SPLIT)]
        for t in range(tiles):
            rows = []
            for first, second in chunks:
                rows += [first_of(first, t), first_of(second, t)]
                rows += [last_of(first, t, tiles), last_of(second, t, tiles)]
            rows[-4:] = (rows[-4:-3], rows[-3:-2], rows[-2:])[g]
            xs[128 * g : 128 * g + 128, 128 * t : 128 * t + 128] = jnp.concatenate(rows, axis=0).astype(BF16)

    def project_in(g):
        lhs = xs[128 * g : 128 * g + 128, :]

        @pl.loop(0, 2)
        def _(h):
            cols = pl.ds(pl.multiple_of(h * half, 128), half)
            part = jnp.dot(lhs, win[:, cols], preferred_element_type=F32).reshape(8, 16, half)
            pf[g, :, h] = part
            pb[g, :, h] = part.astype(BF16)

    def b_copy(g, dy, dx):
        there = plane_col(dy, dx)
        d = dy * 4 + dx
        return remote(
            pb.at[g, there // 2, there % 2], rb.at[g, d], b_send.at[g], b_recv.at[g], plane_peer(dy, dx)
        )

    def b_start(g):
        for dy, dx in PLANE:
            start(b_copy(g, dy, dx))

    def b_finish(g):
        total = pf[g, col // 2, col % 2]
        blocks = all_of(rb.at[g, pl.ds(1, 15)], b_send.at[g], b_recv.at[g])
        blocks.wait_recv()
        for dy, dx in PLANE:
            total += rb[g, dy * 4 + dx].astype(F32)
        v = total + b_in[pl.ds(pl.multiple_of((col % 2) * half, 128), half)].reshape(1, half)
        v = 0.5 * v * (1.0 + jnp.tanh(0.7978845608 * (v + 0.044715 * (v * v * v))))
        hid[g, col // 2, col % 2] = v.astype(BF16)

    def c_start(g):
        block = hid.at[g, col // 2, col % 2]
        for dy, dx in PLANE:
            start(remote(block, block, c_send.at[g], c_recv.at[g], plane_peer(dy, dx)))

    def c_wait(g):
        all_of(rb.at[g, pl.ds(1, 15)], c_send.at[g], c_recv.at[g]).wait_recv()

    def plane_sent(g):
        all_of(rb.at[g, pl.ds(1, 15)], b_send.at[g], b_recv.at[g]).wait_send()
        all_of(rb.at[g, pl.ds(1, 15)], c_send.at[g], c_recv.at[g]).wait_send()

    def project_out(g):
        total = jnp.zeros((128, po.shape[1]), F32)
        for h in range(2):
            lhs = hid[g, :, h].reshape(128, half)
            total += jnp.dot(lhs, wout[h * half : (h + 1) * half, :], preferred_element_type=F32)
        po[128 * g : 128 * g + 128, :] = total

    def share(k, core):
        if isinstance(k, int) and k == SPLIT:
            first, rest = 128 * core + 120, 256 + 120
        else:
            first, rest = first_row(k) + 8 * core, first_row(k) + 16
        first, rest = (po[pl.ds(pl.multiple_of(at, 8), 8), :] for at in (first, rest))
        return pack(first, jnp.where(core == 0, rest[0:4], rest[4:8]))

    def d_sibling_one(k):
        return remote(ss.at[k], sr.at[k], ds_send.at[0], ds_recv.at[k], sibling)

    def d_sibling_start_one(k):
        ss[k] = share(k, 1 - c).astype(BF16)
        start(d_sibling_one(k))

    def d_sibling(g):
        part = pl.ds(CHUNKS[g][0], 5)
        return remote(ss.at[part], sr.at[part], ds_send.at[0], ds_recv.at[CHUNKS[g][0]], sibling)

    def d_sibling_start(g):
        for k in range(*CHUNKS[g]):
            ss[k] = share(k, 1 - c).astype(BF16)
        start(d_sibling(g))

    def chip(k):
        return share(k, c) + sr[k].astype(F32)

    def d_copy(side, m):
        dz = (1 - 2 * side) * (m - PARENT_OUT[m])
        place = slot(side, m)
        return remote(zs.at[place], zr.at[place], d_send.at[0], d_recv.at[side, m], z_peer(dz))

    def d_copy8():
        return remote(zs.at[slot(0, 8)], zr.at[slot(0, 8)], d_send.at[0], d_recv.at[0, 8], z_peer(4 * s8))

    def d_sent():
        all_of(sr, ds_send.at[0], ds_recv.at[0]).wait_send()
        all_of(zr.at[pl.ds(0, 15)], d_send.at[0], ds_recv.at[0]).wait_send()

    def d_send_on(side, m, below=()):
        place = slot(side, m)
        total = chip(place)
        for n in below:
            if n == 8:
                d_copy8().wait_recv()
                total += zr[slot(0, 8)].astype(F32)
            else:
                d_copy(side, n).wait_recv()
                total += zr[slot(side, n)].astype(F32)
        zs[place] = total.astype(BF16)
        start(d_copy(side, m))

    for m in (5, 1, 2):
        for side in (0, 1):
            start(a_copy(side, m, OWN))
    start(a_copy(1, 3, OWN))
    a_sibling(2, OWN)
    for m in (1, 2):
        for side in (0, 1):
            a_take(side, m)
    start(a_copy(0, 3, slot(0, 2)))
    for side in (0, 1):
        a_wait(side, 5)
        start(a_copy(side, 4, slot(side, 5)))
    start(a_copy8())
    for m in (7, 6):
        for side in (0, 1):
            start(a_copy(side, m, slot(side, 5)))
    a_take(1, 3)
    for side in (0, 1):
        a_sibling(0, slot(side, 5))
    load_in.wait()
    load_b_in.wait()
    load_b_out.wait()
    a_sibling_wait(2)
    assemble(2)
    project_in(2)
    b_start(2)
    a_take(0, 3)
    for side in (0, 1):
        a_take(side, 4)
    a_sibling_wait(0)
    assemble(0)
    project_in(0)
    b_start(0)
    for m in (6, 7):
        for side in (0, 1):
            a_take(side, m)
    a_copy8().wait_recv()
    a_sibling(1, slot(0, 8))
    a_sibling_wait(1)
    assemble(1)
    project_in(1)
    b_start(1)
    load_out.wait()
    a_sent()
    b_finish(2)
    b_finish(0)
    c_start(0)
    b_finish(1)
    c_start(1)
    c_wait(0)
    project_out(0)
    d_sibling_start(0)
    c_start(2)
    d_sibling(0).wait_recv()
    for side in (0, 1):
        d_send_on(side, 5)
    d_send_on(0, 3)
    c_wait(1)
    project_out(1)
    for k in (slot(0, 8), slot(0, 7), slot(1, 7), slot(0, 6), slot(1, 6)):
        d_sibling_start_one(k)
    d_sibling_one(slot(0, 8)).wait_recv()
    zs[slot(0, 8)] = chip(slot(0, 8)).astype(BF16)
    start(d_copy8())
    for m in (7, 6):
        for side in (0, 1):
            d_sibling_one(slot(side, m)).wait_recv()
            d_send_on(side, m)
    c_wait(2)
    project_out(2)
    d_sibling_start_one(SPLIT)
    d_sibling_start(2)
    d_send_on(1 - c, 4, (5, 6, 7))
    d_send_on(c, 4, (5, 6, 7, 8))
    d_sibling_one(SPLIT).wait_recv()
    d_send_on(1, 3)
    d_sibling(2).wait_recv()
    for m in (2, 1):
        for side in (0, 1):
            d_send_on(side, m)
    for g in range(GROUPS):
        plane_sent(g)
    total = chip(OWN)
    for m in (1, 2, 3, 4):
        for side in (0, 1):
            d_copy(side, m).wait_recv()
            total += zr[slot(side, m)].astype(F32)
    first = jnp.concatenate([first_of(total, t) for t in range(tiles)], axis=1)
    last = jnp.concatenate([last_of(total, t, tiles) for t in range(tiles)], axis=1)
    out = jnp.concatenate([first, last], axis=0) + b_out[...].reshape(1, -1)
    o_ref[...] = out.astype(BF16)
    d_sent()


def on_device(tokens, w_in, b_in, w_out, b_out):
    width, hidden = w_in.shape
    half = hidden // 2
    chunk = packed_rows(width // 128)
    vmem = pl.BlockSpec(memory_space=pltpu.VMEM)
    hbm = pl.BlockSpec(memory_space=pltpu.HBM)
    dma = pltpu.SemaphoreType.DMA
    return pl.pallas_call(
        kernel,
        out_shape=jax.ShapeDtypeStruct(tokens.shape, BF16),
        in_specs=[hbm] * 5,
        out_specs=vmem,
        scratch_shapes=[
            pltpu.VMEM(tokens.shape, BF16),
            pltpu.VMEM((width, hidden), BF16),
            pltpu.VMEM(b_in.shape, F32),
            pltpu.VMEM((hidden, width), BF16),
            pltpu.VMEM(b_out.shape, F32),
            pltpu.VMEM((2, 16, chunk, 128), BF16),
            pltpu.VMEM((384, width), BF16),
            pltpu.VMEM((GROUPS, 8, 2, 16, half), F32),
            pltpu.VMEM((GROUPS, 8, 2, 16, half), BF16),
            pltpu.VMEM((GROUPS, 16, 16, half), BF16),
            pltpu.VMEM((GROUPS, 8, 2, 16, half), BF16),
            pltpu.VMEM((384, width), F32),
            pltpu.VMEM((16, chunk, 128), BF16),
            pltpu.VMEM((16, chunk, 128), BF16),
            pltpu.VMEM((16, chunk, 128), BF16),
            pltpu.VMEM((16, chunk, 128), BF16),
            dma((5,)),
            dma((1,)), dma((2, 9)),
            dma((1,)), dma((GROUPS,)),
            dma((GROUPS,)), dma((GROUPS,)),
            dma((GROUPS,)), dma((GROUPS,)),
            dma((1,)), dma((16,)),
            dma((1,)), dma((2, 9)),
        ],
        compiler_params=pltpu.CompilerParams(
            collective_id=0, has_side_effects=True, vmem_limit_bytes=60 * 2**20
        ),
        cost_estimate=pl.CostEstimate(
            flops=4 * 384 * width * hidden, bytes_accessed=4 * width * hidden, transcendentals=384 * hidden // 16
        ),
    )(tokens, w_in, b_in, w_out, b_out)


def solution(mesh):
    return jax.shard_map(
        on_device,
        mesh=mesh,
        in_specs=(P("row", "col"), P("col", "row"), P("row"), P("row", "col"), P("col")),
        out_specs=P("row", "col"),
        check_vma=False,
    )
```

```python
import functools

import jax
import jax.numpy as jnp
from jax import lax
from jax.experimental import pallas as pl
from jax.experimental.pallas import tpu as pltpu
from jax.sharding import PartitionSpec as P

BF16 = jnp.bfloat16
F32 = jnp.float32
PARENT = {1: 0, 2: 0, 5: 0, 3: 2, 4: 5, 6: 5, 7: 5, 8: 5}
PARENT_OUT = {1: 0, 2: 0, 3: 0, 4: 0, 5: 0, 6: 5, 7: 5, 8: 5}
SPLIT, OWN = 10, 11
PLANE = [(dy, dx) for dy in (2, 1, 3, 0) for dx in (2, 1, 3, 0) if (dy, dx) != (0, 0)]
GROUPS = 3
CHUNKS = ((0, 5), (5, 10), (11, 16))
PARTS = ((0, 5), (5, 10), (10, 16))


def slot(side, m):
    if m == 3:
        return (2, SPLIT)[side]
    return {5: 0, 4: 3, 8: 5, 7: 6, 6: 8, 1: 12, 2: 14}[m] + side


def pack(first, last):
    tiles = first.shape[1] // 128
    groups = [first[:, 128 * t : 128 * t + 128] for t in range(tiles)]
    ends = [last[:, 128 * t : 128 * t + 128] for t in range(tiles)]
    if tiles % 2:
        ends.append(jnp.zeros_like(ends[0]))
    groups += [jnp.concatenate(ends[t : t + 2], axis=0) for t in range(0, len(ends), 2)]
    if len(groups) % 2:
        groups.append(jnp.zeros_like(groups[0]))
    return jnp.concatenate(groups, axis=0)


def packed_rows(tiles):
    groups = tiles + (tiles + 1) // 2
    return 8 * (groups + groups % 2)


def first_of(packed, t):
    return packed[8 * t : 8 * t + 8]


def last_of(packed, t, tiles):
    at = 8 * (tiles + t // 2) + 4 * (t % 2)
    return packed[at : at + 4]


def first_row(place):
    if not isinstance(place, int):
        return 24 * place
    group = 0 if place < 5 else 1 if place < 10 else 2
    return 128 * group + 24 * (place - CHUNKS[group][0])


def kernel(
    tok_hbm, win_ref, bin_hbm, wout_ref, bout_hbm, o_ref,
    tok, win, b_in, wout, b_out, ta, xs, pf, pb, rb, hid, po, ss, sr, zs, zr,
    wsem, a_send, a_recv, as_send, as_recv, b_send, b_recv, c_send, c_recv,
    ds_send, ds_recv, d_send, d_recv,
):
    row, col = lax.axis_index("row"), lax.axis_index("col")
    z, c = row // 2, row % 2
    y, x = col // 4, col % 4
    half = pb.shape[-1]
    tiles = xs.shape[1] // 128
    s8 = 1 - 2 * c

    def z_peer(dz):
        return {"row": lax.rem(z + dz + 16, 16) * 2 + c, "col": col}

    def plane_col(dy, dx):
        return lax.rem(y + dy + 4, 4) * 4 + lax.rem(x + dx + 4, 4)

    def plane_peer(dy, dx):
        return {"row": row, "col": plane_col(dy, dx)}

    sibling = {"row": z * 2 + (1 - c), "col": col}

    def remote(src, dst, send, recv, peer):
        return pltpu.make_async_remote_copy(
            src_ref=src, dst_ref=dst, send_sem=send, recv_sem=recv,
            device_id=peer, device_id_type=pl.DeviceIdType.MESH,
        )

    def start(copy):
        copy.start()

    def all_of(block, send, recv):
        return remote(block, block, send, recv, sibling)

    load_tok = pltpu.make_async_copy(tok_hbm, tok, wsem.at[2])
    load_tok.start()

    barrier = pltpu.get_barrier_semaphore()
    peers = [z_peer(dz) for dz in (5, -5, 4, -4, 3, -3, 2, -2, 1, -1)]
    peers += [plane_peer(dy, dx) for dy, dx in PLANE] + [sibling]
    for peer in peers:
        pl.semaphore_signal(barrier, inc=1, device_id=peer, device_id_type=pl.DeviceIdType.MESH)
    load_in = pltpu.make_async_copy(win_ref, win, wsem.at[0])
    load_out = pltpu.make_async_copy(wout_ref, wout, wsem.at[1])
    load_b_in = pltpu.make_async_copy(bin_hbm, b_in, wsem.at[3])
    load_b_out = pltpu.make_async_copy(bout_hbm, b_out, wsem.at[4])
    for load in (load_in, load_out, load_b_in, load_b_out):
        load.start()
    load_tok.wait()

    own = tok[...].astype(F32)
    ta[c, OWN] = pack(own[0:8], own[8:12]).astype(BF16)
    pl.semaphore_wait(barrier, len(peers))

    def a_copy(side, m, at):
        sign = 1 - 2 * side
        dz = -sign * (m - (0 if m == 3 and side == 1 else PARENT[m]))
        place = slot(side, m)
        return remote(ta.at[c, at], ta.at[c, place], a_send.at[0], a_recv.at[side, m], z_peer(dz))

    def a_copy8():
        return remote(ta.at[c, slot(0, 5) + c], ta.at[c, slot(0, 8)], a_send.at[0], a_recv.at[0, 8], z_peer(-3 * s8))

    def a_wait(side, m):
        a_copy(side, m, 0).wait_recv()

    def a_sibling(g, place):
        start(remote(ta.at[c, place], ta.at[c, place], as_send.at[0], as_recv.at[g], sibling))

    def a_sibling_wait(g):
        part = pl.ds(PARTS[g][0], PARTS[g][1] - PARTS[g][0])
        all_of(ta.at[1 - c, part], as_send.at[0], as_recv.at[g]).wait_recv()

    def a_take(side, m):
        a_wait(side, m)
        place = slot(side, m)
        a_sibling(0 if place < 5 else 1 if place < 10 else 2, place)

    def a_sent():
        all_of(ta.at[c, pl.ds(0, 15)], a_send.at[0], as_recv.at[0]).wait_send()
        all_of(ta.at[c], as_send.at[0], as_recv.at[0]).wait_send()

    def assemble(g):
        chunks = [(ta[0, k].astype(F32), ta[1, k].astype(F32)) for k in (*range(*CHUNKS[g]), SPLIT)]
        for t in range(tiles):
            rows = []
            for first, second in chunks:
                rows += [first_of(first, t), first_of(second, t)]
                rows += [last_of(first, t, tiles), last_of(second, t, tiles)]
            rows[-4:] = (rows[-4:-3], rows[-3:-2], rows[-2:])[g]
            xs[128 * g : 128 * g + 128, 128 * t : 128 * t + 128] = jnp.concatenate(rows, axis=0).astype(BF16)

    def project_in(g):
        lhs = xs[128 * g : 128 * g + 128, :]

        @pl.loop(0, 2)
        def _(h):
            cols = pl.ds(pl.multiple_of(h * half, 128), half)
            part = jnp.dot(lhs, win[:, cols], preferred_element_type=F32).reshape(8, 16, half)
            pf[g, :, h] = part
            pb[g, :, h] = part.astype(BF16)

    def b_copy(g, dy, dx):
        there = plane_col(dy, dx)
        d = dy * 4 + dx
        return remote(
            pb.at[g, there // 2, there % 2], rb.at[g, d], b_send.at[g], b_recv.at[g], plane_peer(dy, dx)
        )

    def b_start(g):
        for dy, dx in PLANE:
            start(b_copy(g, dy, dx))

    def b_finish(g):
        total = pf[g, col // 2, col % 2]
        blocks = all_of(rb.at[g, pl.ds(1, 15)], b_send.at[g], b_recv.at[g])
        blocks.wait_recv()
        for dy, dx in PLANE:
            total += rb[g, dy * 4 + dx].astype(F32)
        v = total + b_in[pl.ds(pl.multiple_of((col % 2) * half, 128), half)].reshape(1, half)
        v = 0.5 * v * (1.0 + jnp.tanh(0.7978845608 * (v + 0.044715 * (v * v * v))))
        hid[g, col // 2, col % 2] = v.astype(BF16)

    def c_start(g):
        block = hid.at[g, col // 2, col % 2]
        for dy, dx in PLANE:
            start(remote(block, block, c_send.at[g], c_recv.at[g], plane_peer(dy, dx)))

    def c_wait(g):
        all_of(rb.at[g, pl.ds(1, 15)], c_send.at[g], c_recv.at[g]).wait_recv()

    def plane_sent(g):
        all_of(rb.at[g, pl.ds(1, 15)], b_send.at[g], b_recv.at[g]).wait_send()
        all_of(rb.at[g, pl.ds(1, 15)], c_send.at[g], c_recv.at[g]).wait_send()

    def project_out(g):
        total = jnp.zeros((128, po.shape[1]), F32)
        for h in range(2):
            lhs = hid[g, :, h].reshape(128, half)
            total += jnp.dot(lhs, wout[h * half : (h + 1) * half, :], preferred_element_type=F32)
        po[128 * g : 128 * g + 128, :] = total

    def share(k, core):
        if isinstance(k, int) and k == SPLIT:
            first, rest = 128 * core + 120, 256 + 120
        else:
            first, rest = first_row(k) + 8 * core, first_row(k) + 16
        first, rest = (po[pl.ds(pl.multiple_of(at, 8), 8), :] for at in (first, rest))
        return pack(first, jnp.where(core == 0, rest[0:4], rest[4:8]))

    def d_sibling_one(k):
        return remote(ss.at[k], sr.at[k], ds_send.at[0], ds_recv.at[k], sibling)

    def d_sibling_start_one(k):
        ss[k] = share(k, 1 - c).astype(BF16)
        start(d_sibling_one(k))

    def d_sibling(g):
        part = pl.ds(CHUNKS[g][0], 5)
        return remote(ss.at[part], sr.at[part], ds_send.at[0], ds_recv.at[CHUNKS[g][0]], sibling)

    def d_sibling_start(g):
        for k in range(*CHUNKS[g]):
            ss[k] = share(k, 1 - c).astype(BF16)
        start(d_sibling(g))

    def chip(k):
        return share(k, c) + sr[k].astype(F32)

    def d_copy(side, m):
        dz = (1 - 2 * side) * (m - PARENT_OUT[m])
        place = slot(side, m)
        return remote(zs.at[place], zr.at[place], d_send.at[0], d_recv.at[side, m], z_peer(dz))

    def d_copy8():
        return remote(zs.at[slot(0, 8)], zr.at[slot(0, 8)], d_send.at[0], d_recv.at[0, 8], z_peer(3 * s8))

    def d_sent():
        all_of(sr, ds_send.at[0], ds_recv.at[0]).wait_send()
        all_of(zr.at[pl.ds(0, 15)], d_send.at[0], ds_recv.at[0]).wait_send()

    def d_send_on(side, m, below=()):
        place = slot(side, m)
        total = chip(place)
        for n in below:
            if n == 8:
                d_copy8().wait_recv()
                total += zr[slot(0, 8)].astype(F32)
            else:
                d_copy(side, n).wait_recv()
                total += zr[slot(side, n)].astype(F32)
        zs[place] = total.astype(BF16)
        start(d_copy(side, m))

    for m in (5, 1, 2):
        for side in (0, 1):
            start(a_copy(side, m, OWN))
    start(a_copy(1, 3, OWN))
    a_sibling(2, OWN)
    for m in (1, 2):
        for side in (0, 1):
            a_take(side, m)
    start(a_copy(0, 3, slot(0, 2)))
    for side in (0, 1):
        a_wait(side, 5)
        start(a_copy(side, 4, slot(side, 5)))
    start(a_copy8())
    for m in (7, 6):
        for side in (0, 1):
            start(a_copy(side, m, slot(side, 5)))
    a_take(1, 3)
    for side in (0, 1):
        a_sibling(0, slot(side, 5))
    load_in.wait()
    load_b_in.wait()
    load_b_out.wait()
    a_sibling_wait(2)
    assemble(2)
    project_in(2)
    b_start(2)
    a_take(0, 3)
    for side in (0, 1):
        a_take(side, 4)
    a_sibling_wait(0)
    assemble(0)
    project_in(0)
    b_start(0)
    for m in (6, 7):
        for side in (0, 1):
            a_take(side, m)
    a_copy8().wait_recv()
    a_sibling(1, slot(0, 8))
    a_sibling_wait(1)
    assemble(1)
    project_in(1)
    b_start(1)
    load_out.wait()
    a_sent()
    b_finish(2)
    b_finish(0)
    c_start(0)
    b_finish(1)
    c_start(1)
    c_start(2)
    c_wait(0)
    project_out(0)
    d_sibling_start(0)
    d_sibling(0).wait_recv()
    for side in (0, 1):
        d_send_on(side, 4)
    d_send_on(0, 3)
    c_wait(1)
    project_out(1)
    for k in (slot(0, 8), slot(0, 7), slot(1, 7), slot(0, 6), slot(1, 6)):
        d_sibling_start_one(k)
    d_sibling_one(slot(0, 8)).wait_recv()
    zs[slot(0, 8)] = chip(slot(0, 8)).astype(BF16)
    start(d_copy8())
    for m in (7, 6):
        for side in (0, 1):
            d_sibling_one(slot(side, m)).wait_recv()
            d_send_on(side, m)
    c_wait(2)
    project_out(2)
    d_sibling_start_one(SPLIT)
    d_sibling_start(2)
    d_send_on(1 - c, 5, (6, 7))
    d_send_on(c, 5, (6, 7, 8))
    d_sibling_one(SPLIT).wait_recv()
    d_send_on(1, 3)
    d_sibling(2).wait_recv()
    for m in (2, 1):
        for side in (0, 1):
            d_send_on(side, m)
    for g in range(GROUPS):
        plane_sent(g)
    total = chip(OWN)
    for m in (1, 2, 3, 4, 5):
        for side in (0, 1):
            d_copy(side, m).wait_recv()
            total += zr[slot(side, m)].astype(F32)
    first = jnp.concatenate([first_of(total, t) for t in range(tiles)], axis=1)
    last = jnp.concatenate([last_of(total, t, tiles) for t in range(tiles)], axis=1)
    out = jnp.concatenate([first, last], axis=0) + b_out[...].reshape(1, -1)
    o_ref[...] = out.astype(BF16)
    d_sent()


def on_device(tokens, w_in, b_in, w_out, b_out):
    width, hidden = w_in.shape
    half = hidden // 2
    chunk = packed_rows(width // 128)
    vmem = pl.BlockSpec(memory_space=pltpu.VMEM)
    hbm = pl.BlockSpec(memory_space=pltpu.HBM)
    dma = pltpu.SemaphoreType.DMA
    return pl.pallas_call(
        kernel,
        out_shape=jax.ShapeDtypeStruct(tokens.shape, BF16),
        in_specs=[hbm] * 5,
        out_specs=vmem,
        scratch_shapes=[
            pltpu.VMEM(tokens.shape, BF16),
            pltpu.VMEM((width, hidden), BF16),
            pltpu.VMEM(b_in.shape, F32),
            pltpu.VMEM((hidden, width), BF16),
            pltpu.VMEM(b_out.shape, F32),
            pltpu.VMEM((2, 16, chunk, 128), BF16),
            pltpu.VMEM((384, width), BF16),
            pltpu.VMEM((GROUPS, 8, 2, 16, half), F32),
            pltpu.VMEM((GROUPS, 8, 2, 16, half), BF16),
            pltpu.VMEM((GROUPS, 16, 16, half), BF16),
            pltpu.VMEM((GROUPS, 8, 2, 16, half), BF16),
            pltpu.VMEM((384, width), F32),
            pltpu.VMEM((16, chunk, 128), BF16),
            pltpu.VMEM((16, chunk, 128), BF16),
            pltpu.VMEM((16, chunk, 128), BF16),
            pltpu.VMEM((16, chunk, 128), BF16),
            dma((5,)),
            dma((1,)), dma((2, 9)),
            dma((1,)), dma((GROUPS,)),
            dma((GROUPS,)), dma((GROUPS,)),
            dma((GROUPS,)), dma((GROUPS,)),
            dma((1,)), dma((16,)),
            dma((1,)), dma((2, 9)),
        ],
        compiler_params=pltpu.CompilerParams(
            collective_id=0, has_side_effects=True, vmem_limit_bytes=60 * 2**20
        ),
        cost_estimate=pl.CostEstimate(
            flops=4 * 384 * width * hidden, bytes_accessed=4 * width * hidden, transcendentals=384 * hidden // 16
        ),
    )(tokens, w_in, b_in, w_out, b_out)


def solution(mesh):
    return jax.shard_map(
        on_device,
        mesh=mesh,
        in_specs=(P("row", "col"), P("col", "row"), P("row"), P("row", "col"), P("col")),
        out_specs=P("row", "col"),
        check_vma=False,
    )
```
